256 devices in a mesh: row: 8 (over z_hi, y), col: 32 (over x, z_lo, core).
Axes of the slice: x: 4, y: 4, z: 8 (z_hi: 2, z_lo: 4; z = z_hi * 4 + z_lo), core: 2. Of those that a mesh axis runs over, the one named last changes fastest.
Arguments:
- features: bfloat16 [524288, 256], P(('row', 'col')), may hold values from -6 to 6
- tile_values: bfloat16 [65536, 128, 128], P(('row', 'col')), as said below
- tile_rows: int32 [65536], P(('row', 'col')), may hold values from 0 to 511, as said below
- tile_cols: int32 [65536], P(('row', 'col')), may hold values from 0 to 127, as said below
- tile_count: int32 [256], P(('row', 'col')), may hold values from 64 to 256, as said below
- weight: bfloat16 [256, 256], replicated, may hold values from -0.375 to 0.375
- bias: float32 [256], replicated, may hold values from -3 to 3
Outputs:
- activated: bfloat16 [524288, 256], P(('row', 'col'))
The draws below stay inside these ranges and needn't reach their ends.
Inputs may be any that keep to these rules, and one draw needn't show every extreme that they name: tile_count[d] is the number of live slots of cell d, the first ones of its 256; the largest entry equals 256 in every draw, and every entry is 256, 128 or 64. `tile_values`: nonnegative edge weights. With P = 16, in grid cell d = r * 32 + c: an even slot 2 m has tile_rows // P == c, and an odd slot 2 m + 1 has tile_rows // P == m % 32. With P = 16, in grid cell d = r * 32 + c: an even slot has tile_cols // P == r and tile_cols % P within one of its tile_rows % P.
All inputs are finite; a program needn't handle non-finite values.
Results may differ from the reference program's by a relative error of at most 0.0047.
Values may be sent and summed in bfloat16 or wider, within the bound.
A program may use at most 128 MiB of HBM per device.

```python
import jax
import jax.numpy as jnp
from jax import lax

F = 256
BLOCK = 128
ROWS_DEV = 2048
SLOTS = 256
NODES = 524288
IN_BLOCKS = 128
TILE_SLOTS = 65536
N_ROW = 8
N_COL = 32


def tile_layout(key):
    blocks_here = ROWS_DEV // BLOCK
    slot_index = jnp.arange(TILE_SLOTS, dtype=jnp.int32)
    cell_index = slot_index // SLOTS
    grid_row = cell_index // N_COL
    grid_col = cell_index % N_COL
    within = slot_index % SLOTS
    pair_number = within // 2
    local_row = jax.random.randint(jax.random.fold_in(key, 21), (TILE_SLOTS,), 0, blocks_here)
    offset_draw = jax.random.randint(jax.random.fold_in(key, 22), (TILE_SLOTS,), -1, 2)
    local_col = jnp.clip(local_row + offset_draw, 0, blocks_here - 1)
    random_col = jax.random.randint(jax.random.fold_in(key, 23), (TILE_SLOTS,), 0, IN_BLOCKS)
    diagonal = within % 2 == 0
    rows_out = jnp.where(diagonal, grid_col * blocks_here + local_row, pair_number % N_COL * blocks_here + local_row)
    cols_out = jnp.where(diagonal, grid_row * blocks_here + local_col, random_col)
    return (rows_out.astype(jnp.int32), cols_out.astype(jnp.int32))


def draw_tile_rows(key, part):
    return tile_layout(key)[0]


def draw_tile_cols(key, part):
    return tile_layout(key)[1]


def draw_tile_values(key, part):
    live_terms = SLOTS * 7.0 / 12.0 / (ROWS_DEV // BLOCK) * BLOCK
    top_value = (3.0 / live_terms) ** 0.5
    uniform_part = jax.random.uniform(jax.random.fold_in(key, 7), (TILE_SLOTS, BLOCK, BLOCK), jnp.float32)
    return (uniform_part * top_value).astype(jnp.bfloat16)


def draw_tile_count(key, part):
    cell_total = N_ROW * N_COL
    shifts = jax.random.randint(jax.random.fold_in(key, 11), (cell_total,), 0, 3)
    counts = jnp.right_shift(jnp.full((cell_total,), SLOTS, jnp.int32), shifts)
    busiest = jax.random.randint(jax.random.fold_in(key, 13), (), 0, cell_total)
    return jnp.where(jnp.arange(cell_total) == busiest, SLOTS, counts).astype(jnp.int32)


def block_scale(own_key, dims, shards, least, high):
    gain = 1.0
    for dim, blocks in shards:
        steps = jax.random.uniform(jax.random.fold_in(jax.random.fold_in(own_key, 6), dim), (blocks,), jnp.float32, least / len(shards), high / len(shards))
        gain = gain * jnp.repeat(jnp.exp(steps), dims[dim] // blocks).reshape((-1,) + (1,) * (len(dims) - 1 - dim))
    return gain


def noise(own_key, extent, scale, bound, shards=(), held_as=jnp.bfloat16):
    entries = scale * jax.random.normal(own_key, extent, jnp.float32)
    if shards:
        entries = entries * block_scale(own_key, extent, shards, -0.22, 0.18)
    return jnp.clip(entries, -bound, bound).astype(held_as)


def setup_inputs(seed: int = 0) -> dict:
    key_list = jax.random.split(jax.random.key(seed), 8)
    return {
        "features": noise(key_list[0], (NODES, F), 1.0, 6.0, ((0, 256),)),
        "tile_values": draw_tile_values(jax.random.fold_in(key_list[7], 71), 0),
        "tile_rows": draw_tile_rows(jax.random.fold_in(key_list[7], 71), 0),
        "tile_cols": draw_tile_cols(jax.random.fold_in(key_list[7], 71), 0),
        "tile_count": draw_tile_count(jax.random.fold_in(key_list[7], 71), 0),
        "weight": noise(key_list[5], (F, F), F ** -0.5, 0.375),
        "bias": noise(key_list[6], (F,), 0.5, 3.0, (), jnp.float32),
    }


def reference(features, tile_values, tile_rows, tile_cols, tile_count, weight, bias):
    per_dev = ROWS_DEV // BLOCK
    cell_total = N_ROW * N_COL
    node_blocks = features.reshape(NODES // BLOCK, BLOCK, F)
    values = tile_values.reshape(cell_total, SLOTS, BLOCK, BLOCK)
    row_ids = tile_rows.reshape(cell_total, SLOTS)
    col_ids = tile_cols.reshape(cell_total, SLOTS)
    slot_ids = jnp.arange(SLOTS, dtype=jnp.int32)

    def one_cell(running, cell):
        cell_values, cell_rows, cell_cols, live_count, cell_index = cell
        grid_row = cell_index // N_COL
        grid_col = cell_index % N_COL
        out_global = (grid_row * N_COL * per_dev + cell_rows).astype(jnp.int32)
        in_global = (((cell_cols // per_dev) * N_COL + grid_col) * per_dev + cell_cols % per_dev).astype(jnp.int32)
        sources = node_blocks[in_global].astype(jnp.float32)
        product = jnp.einsum("sij,sjf->sif", cell_values.astype(jnp.float32), sources)
        live_mask = (slot_ids < live_count).astype(jnp.float32)
        return running.at[out_global].add(product * live_mask[:, None, None]), None

    start_sum = jnp.zeros((NODES // BLOCK, BLOCK, F), jnp.float32)
    running, _ = lax.scan(one_cell, start_sum, (values, row_ids, col_ids, tile_count, jnp.arange(cell_total, dtype=jnp.int32)))
    aggregated = running.reshape(NODES, F).astype(jnp.bfloat16)
    projected = jnp.dot(aggregated, weight, preferred_element_type=jnp.float32) + bias
    return jnp.maximum(projected, 0.0).astype(jnp.bfloat16)
```

```python
import jax
import jax.numpy as jnp
from jax import lax
from jax.experimental import pallas as pl
from jax.experimental.pallas import tpu as pltpu
from jax.sharding import PartitionSpec as P

MESH = pl.DeviceIdType.MESH
BLOCK = 128
PER_DEV = 16
PAIRS = 128
HALF = 128
ROWS = PER_DEV * BLOCK
GROUP = 16
N_X, N_Z, N_Y, N_HI = 4, 4, 4, 2
LEVELS = 4
CHUNK = 16


def near_kernel(row_ref, col_ref, live_ref, feat_ref, tiles_ref, acc_ref, held, sem):
    live = live_ref[0]
    copies = [
        pltpu.make_async_copy(
            tiles_ref.at[pl.ds(c * CHUNK, CHUNK), 0], held.at[pl.ds(c * CHUNK, CHUNK)], sem.at[c]
        )
        for c in range(PAIRS // CHUNK)
    ]
    for c, copy in enumerate(copies):
        pl.when(c * CHUNK < live)(copy.start)
    acc_ref[...] = jnp.zeros_like(acc_ref)
    for c, copy in enumerate(copies):

        @pl.when(c * CHUNK < live)
        def _():
            copy.wait()

            def add(s, carry):
                slot = c * CHUNK + s
                out = pl.ds(pl.multiple_of(row_ref[slot] * BLOCK, BLOCK), BLOCK)
                src = pl.ds(pl.multiple_of(col_ref[slot] * BLOCK, BLOCK), BLOCK)
                acc_ref[out, :] += jnp.dot(
                    held[slot], feat_ref[src, :], preferred_element_type=jnp.float32
                )
                return carry

            lax.fori_loop(0, CHUNK, add, 0, unroll=4)


def near(row_ids, col_ids, live, features, tiles):
    vmem = pl.BlockSpec(memory_space=pltpu.VMEM)
    smem = pl.BlockSpec(memory_space=pltpu.SMEM)
    return pl.pallas_call(
        near_kernel,
        out_shape=jax.ShapeDtypeStruct((ROWS, 2 * HALF), jnp.float32),
        in_specs=[smem, smem, smem, vmem, pl.BlockSpec(memory_space=pl.ANY)],
        out_specs=vmem,
        scratch_shapes=[
            pltpu.VMEM((PAIRS, BLOCK, BLOCK), jnp.bfloat16),
            pltpu.SemaphoreType.DMA((PAIRS // CHUNK,)),
        ],
        compiler_params=pltpu.CompilerParams(vmem_limit_bytes=24 * 2**20),
    )(row_ids, col_ids, live, features, tiles)


def far_kernel(
    src_ref,
    feat_ref,
    ids_ref,
    weight_ref,
    bias_ref,
    tiles_ref,
    near_ref,
    out_ref,
    gath0,
    gath1,
    tiles,
    ids,
    pick,
    xs,
    xr,
    zs,
    zr,
    own,
    near_sum,
    proj,
    tile_sem,
    near_sem,
    hi_send,
    hi_recv,
    y_send,
    y_recv,
    id_send,
    id_recv,
    x_send,
    x_recv,
    z_send,
    z_recv,
):
    row = lax.axis_index("row")
    col = lax.axis_index("col")
    z_hi, y = row // N_Y, lax.rem(row, N_Y)
    x, z, k = col // (2 * N_Z), lax.rem(col // 2, N_Z), lax.rem(col, 2)
    mine = x * 2 + k
    gath = (gath0, gath1)

    def plane(o):
        return lax.rem(x + o // 2, N_X) * 2 + lax.rem(k + lax.rem(o, 2), 2)

    def plane_dev(p):
        return {"row": row, "col": (p // 2) * (2 * N_Z) + z * 2 + lax.rem(p, 2)}

    def y_dev(d):
        return {"row": z_hi * N_Y + lax.rem(y + d, N_Y), "col": col}

    hi_row = (1 - z_hi) * N_Y + y
    hi_dev = {"row": hi_row, "col": col}

    def z_dev(d):
        return {"row": row, "col": x * (2 * N_Z) + lax.rem(z + d, N_Z) * 2 + k}

    load_tiles = pltpu.make_async_copy(tiles_ref.at[:, 1], tiles, tile_sem)
    load_tiles.start()
    load_near = pltpu.make_async_copy(near_ref, near_sum, near_sem)
    load_near.start()

    barrier = pltpu.get_barrier_semaphore()
    peers = [hi_dev] + [y_dev(d) for d in range(1, N_Y)] + [z_dev(d) for d in range(1, N_Z)]
    peers += [plane_dev(plane(o)) for o in range(1, 8)]
    for peer in peers:
        pl.semaphore_signal(barrier, inc=1, device_id=peer, device_id_type=MESH)
    pl.semaphore_wait(barrier, len(peers))

    def share(h, r):
        return gath[h].at[pl.ds(r * PER_DEV, PER_DEV)]

    def copy(src, dst, send, recv, peer):
        return pltpu.make_async_remote_copy(
            src_ref=src, dst_ref=dst, send_sem=send, recv_sem=recv, device_id=peer, device_id_type=MESH
        )

    def hi_copy(h):
        half = feat_ref.at[:, :, pl.ds(h * HALF, HALF)]
        return copy(half, share(h, row), hi_send.at[h], hi_recv.at[h], hi_dev)

    def y_copy(h, d, part):
        src = feat_ref.at[:, :, pl.ds(h * HALF, HALF)] if part == 0 else share(h, hi_row)
        dst = share(h, row if part == 0 else hi_row)
        sems = y_send.at[h, part, d - 1], y_recv.at[h, part, d - 1]
        return copy(src, dst, *sems, y_dev(d))

    def y_arrival(h, d, part):
        back = lax.rem(y + N_Y - d, N_Y)
        r = (z_hi if part == 0 else 1 - z_hi) * N_Y + back
        sems = y_send.at[h, part, d - 1], y_recv.at[h, part, d - 1]
        return copy(share(h, r), share(h, r), *sems, y_dev(d))

    def hi_arrival(h):
        dst = share(h, hi_row)
        return copy(dst, dst, hi_send.at[h], hi_recv.at[h], hi_dev)

    def id_copy(o):
        p = plane(o)
        return copy(ids_ref.at[p], ids.at[mine], id_send.at[p], id_recv.at[mine], plane_dev(p))

    def id_arrival(o):
        p = plane(o)
        return copy(ids.at[p], ids.at[p], id_send.at[p], id_recv.at[p], plane_dev(p))

    def x_copy(h, j, o):
        p = plane(o)
        return copy(xs.at[h, j, o - 1], xr.at[h, j, mine], x_send.at[h, j, p], x_recv.at[h, j, mine], plane_dev(p))

    def x_arrival(h, j, o):
        p = plane(o)
        return copy(xr.at[h, j, p], xr.at[h, j, p], x_send.at[h, j, p], x_recv.at[h, j, p], plane_dev(p))

    def z_copy(h, j):
        return copy(zs.at[h, j], zr.at[h, j], z_send.at[h, j], z_recv.at[h, j], z_dev(j + 1))

    def over(n, body):
        def step(o, carry):
            body(o)
            return carry

        lax.fori_loop(1, n, step, 0)

    hi_copy(0).start()
    for d in (1, 3, 2):
        y_copy(0, d, 0).start()
    over(8, lambda o: id_copy(o).start())
    for h in range(2):
        for b in range(PER_DEV):
            gath[h][row * PER_DEV + b] = feat_ref[b, :, pl.ds(h * HALF, HALF)]
        gath[h][8 * PER_DEV] = jnp.zeros((BLOCK, HALF), jnp.bfloat16)
    ids[mine] = ids_ref[mine]

    over(8, lambda o: id_arrival(o).wait_recv())

    def build(j):
        to = lax.rem(z + 1 + j, N_Z)
        line = lax.broadcasted_iota(jnp.int32, (PER_DEV * GROUP, BLOCK), 0)
        lane = lax.broadcasted_iota(jnp.int32, (PER_DEV * GROUP, BLOCK), 1)
        same = lax.rem(line, GROUP) == lax.rem(lane, GROUP)
        for c in range(N_X):
            block = ids[2 * c, pl.ds(to, 1), :] + ids[2 * c + 1, pl.ds(to, 1), :]
            hit = same & (line // GROUP == block)
            pick[j, :, pl.ds(c * BLOCK, BLOCK)] = jnp.where(hit, 1.0, 0.0).astype(jnp.bfloat16)

    for j in range(N_Z):
        build(j)

    hi_arrival(0).wait_recv()
    for d in (1, 3, 2):
        y_copy(0, d, 1).start()
    hi_copy(1).start()
    load_tiles.wait()
    for d in (1, 3, 2):
        y_arrival(0, d, 0).wait_recv()
    for d in (1, 3, 2):
        y_arrival(0, d, 1).wait_recv()
    for d in (1, 3, 2):
        y_copy(1, d, 0).start()

    def product(h, j, p, lv):
        to = lax.rem(z + 1 + j, N_Z)
        slot = lv * 32 + (p // 2) * (2 * N_Z) + to * 2 + lax.rem(p, 2)
        out = jnp.dot(tiles[slot], gath[h][src_ref[slot]], preferred_element_type=jnp.float32)
        return out.astype(jnp.bfloat16)

    def multiply(h, j):
        def one(o):
            for lv in range(LEVELS):
                xs[h, j, o - 1, lv] = product(h, j, plane(o), lv)
            x_copy(h, j, o).start()

        over(8, one)
        for lv in range(LEVELS):
            xr[h, j, mine, lv] = product(h, j, mine, lv)

    def combine(h, j):
        over(8, lambda o: x_arrival(h, j, o).wait_recv())

        def some(g, carry):
            rows = pl.ds(pl.multiple_of(g * GROUP, GROUP), GROUP)
            arrived = xr[h, j, :, :, rows, :].reshape(8 * LEVELS * GROUP, HALF)
            total = jnp.dot(pick[j], arrived, preferred_element_type=jnp.float32)
            total = total.reshape(PER_DEV, GROUP, HALF)
            if j < N_Z - 1:
                zs[h, j, :, rows, :] = total.astype(jnp.bfloat16)
            else:
                own[h, :, rows, :] = total
            return carry

        lax.fori_loop(0, BLOCK // GROUP, some, 0)
        if j < N_Z - 1:
            z_copy(h, j).start()

    def finish(h):
        for j in range(N_Z - 1):
            z_copy(h, j).wait_recv()

        def some(b, carry):
            total = own[h, b] + near_sum[pl.ds(pl.multiple_of(b * BLOCK, BLOCK), BLOCK), pl.ds(h * HALF, HALF)]
            for j in range(N_Z - 1):
                total += zr[h, j, b].astype(jnp.float32)
            part = jnp.dot(
                total.astype(jnp.bfloat16),
                weight_ref[pl.ds(h * HALF, HALF), :],
                preferred_element_type=jnp.float32,
            )
            rows = pl.ds(pl.multiple_of(b * BLOCK, BLOCK), BLOCK)
            if h == 0:
                proj[rows, :] = part
            else:
                out_ref[rows, :] = jnp.maximum(proj[rows, :] + part + bias_ref[...], 0.0).astype(jnp.bfloat16)
            return carry

        lax.fori_loop(0, PER_DEV, some, 0)

    multiply(0, 0)
    multiply(0, 1)
    hi_arrival(1).wait_recv()
    for d in (1, 3, 2):
        y_copy(1, d, 1).start()
    multiply(0, 2)
    multiply(0, 3)
    for j in range(N_Z - 1):
        combine(0, j)
    for part in range(2):
        for d in (1, 3, 2):
            y_arrival(1, d, part).wait_recv()
    for j in range(N_Z):
        multiply(1, j)
    combine(0, 3)
    load_near.wait()
    combine(1, 0)
    combine(1, 1)
    finish(0)
    combine(1, 2)
    combine(1, 3)
    finish(1)

    over(8, lambda o: id_copy(o).wait_send())
    for h in range(2):
        hi_copy(h).wait_send()
        for part in range(2):
            for d in (1, 3, 2):
                y_copy(h, d, part).wait_send()
        for j in range(N_Z):
            over(8, lambda o: x_copy(h, j, o).wait_send())
        for j in range(N_Z - 1):
            z_copy(h, j).wait_send()


def far(src_blocks, features, ids, weight, bias, tiles, near_sum):
    vmem = pl.BlockSpec(memory_space=pltpu.VMEM)
    smem = pl.BlockSpec(memory_space=pltpu.SMEM)
    hbm = pl.BlockSpec(memory_space=pl.ANY)
    dma = pltpu.SemaphoreType.DMA
    return pl.pallas_call(
        far_kernel,
        out_shape=jax.ShapeDtypeStruct((ROWS, 2 * HALF), jnp.bfloat16),
        in_specs=[smem, vmem, vmem, vmem, vmem, hbm, hbm],
        out_specs=vmem,
        scratch_shapes=[
            pltpu.VMEM((8 * PER_DEV + 1, BLOCK, HALF), jnp.bfloat16),
            pltpu.VMEM((8 * PER_DEV + 1, BLOCK, HALF), jnp.bfloat16),
            pltpu.VMEM((PAIRS, BLOCK, BLOCK), jnp.bfloat16),
            pltpu.VMEM((8, 8, BLOCK), jnp.int32),
            pltpu.VMEM((N_Z, PER_DEV * GROUP, 8 * LEVELS * GROUP), jnp.bfloat16),
            pltpu.VMEM((2, N_Z, 7, LEVELS, BLOCK, HALF), jnp.bfloat16),
            pltpu.VMEM((2, N_Z, 8, LEVELS, BLOCK, HALF), jnp.bfloat16),
            pltpu.VMEM((2, N_Z - 1, PER_DEV, BLOCK, HALF), jnp.bfloat16),
            pltpu.VMEM((2, N_Z - 1, PER_DEV, BLOCK, HALF), jnp.bfloat16),
            pltpu.VMEM((2, PER_DEV, BLOCK, HALF), jnp.float32),
            pltpu.VMEM((ROWS, 2 * HALF), jnp.float32),
            pltpu.VMEM((ROWS, 2 * HALF), jnp.float32),
            dma,
            dma,
            dma((2,)),
            dma((2,)),
            dma((2, 2, N_Y - 1)),
            dma((2, 2, N_Y - 1)),
            dma((8,)),
            dma((8,)),
            dma((2, N_Z, 8)),
            dma((2, N_Z, 8)),
            dma((2, N_Z - 1)),
            dma((2, N_Z - 1)),
        ],
        compiler_params=pltpu.CompilerParams(
            collective_id=0, has_side_effects=True, vmem_limit_bytes=56 * 2**20
        ),
    )(src_blocks, features, ids, weight, bias, tiles, near_sum)


def local(features, tile_values, tile_rows, tile_cols, tile_count, weight, bias):
    tiles = tile_values.reshape(PAIRS, 2, BLOCK, BLOCK)
    pair_rows = lax.rem(tile_rows, PER_DEV).reshape(PAIRS, 2)
    pair_cols = tile_cols.reshape(PAIRS, 2)
    near_live = (tile_count + 1) // 2
    near_sum = near(pair_rows[:, 0], lax.rem(pair_cols[:, 0], PER_DEV), near_live, features, tiles)

    pair_index = jnp.arange(PAIRS, dtype=jnp.int32)
    src_blocks = jnp.where(2 * pair_index + 1 < tile_count[0], pair_cols[:, 1], 8 * PER_DEV)
    core = lax.rem(lax.axis_index("col"), 2)
    by_place = pair_rows[:, 1].reshape(LEVELS, N_X, N_Z, 2).transpose(1, 3, 2, 0).reshape(8, N_Z, LEVELS)
    spread = jnp.broadcast_to(by_place[:, :, None, :, None], (8, N_Z, 2, LEVELS, GROUP))
    at_core = (jnp.arange(2, dtype=jnp.int32) == core)[None, None, :, None, None]
    ids = jnp.where(at_core, spread, 0).reshape(8, N_Z, BLOCK)
    ids = jnp.pad(ids, ((0, 0), (0, 8 - N_Z), (0, 0)))
    return far(src_blocks, features.reshape(PER_DEV, BLOCK, -1), ids, weight, bias.reshape(1, -1), tiles, near_sum)


def solution(mesh):
    return jax.shard_map(
        local,
        mesh=mesh,
        in_specs=(
            P(("row", "col"), None),
            P(("row", "col"), None, None),
            P(("row", "col")),
            P(("row", "col")),
            P(("row", "col")),
            P(),
            P(),
        ),
        out_specs=P(("row", "col"), None),
        check_vma=False,
    )
```

```python
import jax
import jax.numpy as jnp
from jax import lax
from jax.experimental import pallas as pl
from jax.experimental.pallas import tpu as pltpu
from jax.sharding import PartitionSpec as P

MESH = pl.DeviceIdType.MESH
BLOCK = 128
PER_DEV = 16
PAIRS = 128
HALF = 128
ROWS = PER_DEV * BLOCK
GROUP = 16
N_X, N_Z, N_Y, N_HI = 4, 4, 4, 2
LEVELS = 4
PART = 64
STEPS = (2, 1, 3, 0)


def far_kernel(
    count_ref,
    col_ref,
    feat_ref,
    rows_ref,
    weight_ref,
    bias_ref,
    tiles_ref,
    out_ref,
    gath0,
    gath1,
    feat,
    near_tiles,
    far_tiles,
    weight,
    bias,
    ids,
    pick,
    near_pick,
    near_prod,
    near_sum,
    xs,
    xr,
    zs,
    zr,
    own,
    proj,
    load_sem,
    share_sem,
    hi_send,
    hi_recv,
    y_send,
    y_recv,
    id_send,
    id_recv,
    x_send,
    x_recv,
    z_send,
    z_recv,
):
    row = lax.axis_index("row")
    col = lax.axis_index("col")
    z_hi, y = row // N_Y, lax.rem(row, N_Y)
    x, z, k = col // (2 * N_Z), lax.rem(col // 2, N_Z), lax.rem(col, 2)
    mine = x * 2 + k
    gath = (gath0, gath1)
    live = count_ref[0]

    def plane(o):
        return lax.rem(x + o // 2, N_X) * 2 + lax.rem(k + lax.rem(o, 2), 2)

    def plane_dev(p):
        return {"row": row, "col": (p // 2) * (2 * N_Z) + z * 2 + lax.rem(p, 2)}

    def y_dev(d):
        return {"row": z_hi * N_Y + lax.rem(y + d, N_Y), "col": col}

    hi_row = (1 - z_hi) * N_Y + y
    hi_dev = {"row": hi_row, "col": col}

    def z_dev(d):
        return {"row": row, "col": x * (2 * N_Z) + lax.rem(z + d, N_Z) * 2 + k}

    loads = [
        pltpu.make_async_copy(src, dst, load_sem.at[i])
        for i, (src, dst) in enumerate(
            (
                (feat_ref, feat.at[pl.ds(0, PER_DEV)]),
                (rows_ref, ids.at[mine]),
                (tiles_ref.at[:, 0], near_tiles),
                (tiles_ref.at[:, 1], far_tiles),
                (weight_ref, weight),
                (bias_ref, bias),
            )
        )
    ]
    load_feat, load_rows, load_near, load_far, load_weight, load_bias = loads
    for load in loads:
        load.start()

    barrier = pltpu.get_barrier_semaphore()
    peers = [hi_dev] + [y_dev(d) for d in range(1, N_Y)] + [z_dev(d) for d in range(1, N_Z)]
    peers += [plane_dev(plane(o)) for o in range(1, 8)]
    for peer in peers:
        pl.semaphore_signal(barrier, inc=1, device_id=peer, device_id_type=MESH)
    feat[PER_DEV] = jnp.zeros((BLOCK, 2 * HALF), jnp.bfloat16)
    for h in range(2):
        gath[h][8 * PER_DEV] = jnp.zeros((BLOCK, HALF), jnp.bfloat16)
    load_feat.wait()
    load_rows.wait()
    pl.semaphore_wait(barrier, len(peers))

    def share(h, r):
        return gath[h].at[pl.ds(r * PER_DEV, PER_DEV)]

    def half(h):
        return feat.at[pl.ds(0, PER_DEV), :, pl.ds(h * HALF, HALF)]

    def copy(src, dst, send, recv, peer):
        return pltpu.make_async_remote_copy(
            src_ref=src, dst_ref=dst, send_sem=send, recv_sem=recv, device_id=peer, device_id_type=MESH
        )

    def hi_copy(h):
        return copy(half(h), share(h, row), hi_send.at[h], hi_recv.at[h], hi_dev)

    def y_copy(h, d, part):
        src = half(h) if part == 0 else share(h, hi_row)
        dst = share(h, row if part == 0 else hi_row)
        sems = y_send.at[h, part, d - 1], y_recv.at[h, part, d - 1]
        return copy(src, dst, *sems, y_dev(d))

    def y_arrival(h, d, part):
        back = lax.rem(y + N_Y - d, N_Y)
        r = (z_hi if part == 0 else 1 - z_hi) * N_Y + back
        sems = y_send.at[h, part, d - 1], y_recv.at[h, part, d - 1]
        return copy(share(h, r), share(h, r), *sems, y_dev(d))

    def hi_arrival(h):
        dst = share(h, hi_row)
        return copy(dst, dst, hi_send.at[h], hi_recv.at[h], hi_dev)

    def id_copy(o):
        p = plane(o)
        return copy(ids.at[mine], ids.at[mine], id_send.at[p], id_recv.at[mine], plane_dev(p))

    def id_arrival(o):
        p = plane(o)
        return copy(ids.at[p], ids.at[p], id_send.at[p], id_recv.at[p], plane_dev(p))

    def levels(u):
        j = min(u, N_Z - 1)
        return (j, range(LEVELS)) if u < N_Z - 1 else (j, range(2 * (u - j), 2 * (u - j) + 2))

    def x_copy(h, u, o):
        p = plane(o)
        j, lvs = levels(u)
        at = pl.ds(lvs[0], len(lvs))
        return copy(
            xs.at[h, j, o - 1, at], xr.at[h, j, mine, at], x_send.at[h, u, p], x_recv.at[h, u, mine], plane_dev(p)
        )

    def x_arrival(h, u, o):
        p = plane(o)
        j, lvs = levels(u)
        dst = xr.at[h, j, p, pl.ds(lvs[0], len(lvs))]
        return copy(dst, dst, x_send.at[h, u, p], x_recv.at[h, u, p], plane_dev(p))

    def z_copy(h, j):
        return copy(zs.at[h, j], zr.at[h, j], z_send.at[h, j], z_recv.at[h, j], z_dev(STEPS[j]))

    def over(n, body):
        def step(o, carry):
            body(o)
            return carry

        lax.fori_loop(1, n, step, 0)

    hi_copy(0).start()
    for d in (1, 3, 2):
        y_copy(0, d, 0).start()
    over(8, lambda o: id_copy(o).start())
    keeps = [pltpu.make_async_copy(half(h), share(h, row), share_sem.at[h]) for h in range(2)]
    for keep in keeps:
        keep.start()

    line = lax.broadcasted_iota(jnp.int32, (PER_DEV * GROUP, BLOCK), 0)
    lane = lax.broadcasted_iota(jnp.int32, (PER_DEV * GROUP, BLOCK), 1)
    same_row = lax.rem(line, GROUP) == lax.rem(lane, GROUP)
    line_block = (line // GROUP).astype(jnp.float32)

    def spread(p, wanted):
        chosen = jnp.where(wanted, 1.0, 0.0).astype(jnp.bfloat16)
        return jnp.dot(ids[p].astype(jnp.bfloat16), chosen, preferred_element_type=jnp.float32)[0:1, :]

    def picker(block):
        return jnp.where(same_row & (line_block == block), 1.0, 0.0).astype(jnp.bfloat16)

    def near(a):
        for c in range(PART * GROUP // BLOCK):
            slot = a * PART + c * (BLOCK // GROUP) + lane // GROUP
            near_pick[:, pl.ds(c * BLOCK, BLOCK)] = picker(spread(mine, line == 2 * slot))

        def multiply_near(s, carry):
            for i in range(4):
                slot = 2 * (a * PART + 4 * s + i)
                src = jnp.where(slot < live, lax.rem(col_ref[slot], PER_DEV), PER_DEV)
                out = jnp.dot(near_tiles[a * PART + 4 * s + i], feat[src], preferred_element_type=jnp.float32)
                near_prod[4 * s + i] = out.astype(jnp.bfloat16)
            return carry

        lax.fori_loop(0, PART // 4, multiply_near, 0)

        def some(g, carry):
            rows = pl.ds(pl.multiple_of(g * GROUP, GROUP), GROUP)
            parts = near_prod[:, rows, :].reshape(PART * GROUP, 2 * HALF)
            total = jnp.dot(near_pick[...], parts, preferred_element_type=jnp.float32)
            total = total.reshape(PER_DEV, GROUP, 2 * HALF)
            near_sum[:, rows, :] = total if a == 0 else near_sum[:, rows, :] + total
            return carry

        lax.fori_loop(0, BLOCK // GROUP, some, 0)

    load_near.wait()
    near(0)
    hi_arrival(0).wait_recv()
    for d in (1, 3, 2):
        y_copy(0, d, 1).start()
    hi_copy(1).start()
    near(1)

    over(8, lambda o: id_arrival(o).wait_recv())
    for j in range(N_Z):
        to = lax.rem(z + STEPS[j], N_Z)
        slot = lax.rem(lane, BLOCK // 2) // GROUP * 32 + x * (2 * N_Z) + to * 2 + k
        for c in range(N_X):
            block = 0.0
            for i in range(2):
                wanted = (line == 2 * slot + 1) & (lane // (BLOCK // 2) == i)
                block += spread(2 * c + i, wanted)
            pick[j, :, pl.ds(c * BLOCK, BLOCK)] = picker(block)

    load_far.wait()
    for keep in keeps:
        keep.wait()
    for part in range(2):
        for d in (1, 3, 2):
            y_arrival(0, d, part).wait_recv()
    for d in (1, 3, 2):
        y_copy(1, d, 0).start()

    def product(h, j, p, lv):
        to = lax.rem(z + STEPS[j], N_Z)
        slot = lv * 32 + (p // 2) * (2 * N_Z) + to * 2 + lax.rem(p, 2)
        src = jnp.where(2 * slot + 1 < live, col_ref[2 * slot + 1], 8 * PER_DEV)
        out = jnp.dot(far_tiles[slot], gath[h][src], preferred_element_type=jnp.float32)
        return out.astype(jnp.bfloat16)

    def multiply(h, u):
        j, lvs = levels(u)

        def one(o):
            for lv in lvs:
                xs[h, j, o - 1, lv] = product(h, j, plane(o), lv)
            x_copy(h, u, o).start()

        over(8, one)
        for lv in lvs:
            xr[h, j, mine, lv] = product(h, j, mine, lv)

    def combine(h, j):
        for u in (j,) if j < N_Z - 1 else (j, j + 1):
            over(8, lambda o: x_arrival(h, u, o).wait_recv())

        def some(g, carry):
            rows = pl.ds(pl.multiple_of(g * GROUP, GROUP), GROUP)
            arrived = xr[h, j, :, :, rows, :].reshape(8 * LEVELS * GROUP, HALF)
            total = jnp.dot(pick[j], arrived, preferred_element_type=jnp.float32)
            total = total.reshape(PER_DEV, GROUP, HALF)
            if j < N_Z - 1:
                zs[h, j, :, rows, :] = total.astype(jnp.bfloat16)
            else:
                own[h, :, rows, :] = total
            return carry

        lax.fori_loop(0, BLOCK // GROUP, some, 0)
        if j < N_Z - 1:
            z_copy(h, j).start()

    def finish(h):
        for j in range(N_Z - 1):
            z_copy(h, j).wait_recv()

        def some(b, carry):
            total = own[h, b] + near_sum[b, :, pl.ds(h * HALF, HALF)]
            for j in range(N_Z - 1):
                total += zr[h, j, b].astype(jnp.float32)
            part = jnp.dot(
                total.astype(jnp.bfloat16),
                weight[pl.ds(h * HALF, HALF), :],
                preferred_element_type=jnp.float32,
            )
            rows = pl.ds(pl.multiple_of(b * BLOCK, BLOCK), BLOCK)
            if h == 0:
                proj[rows, :] = part
            else:
                out_ref[rows, :] = jnp.maximum(proj[rows, :] + part + bias[...], 0.0).astype(jnp.bfloat16)
            return carry

        lax.fori_loop(0, PER_DEV, some, 0)

    multiply(0, 0)
    multiply(0, 1)
    hi_arrival(1).wait_recv()
    for d in (1, 3, 2):
        y_copy(1, d, 1).start()
    multiply(0, 2)
    multiply(0, 3)
    combine(0, 0)
    combine(0, 1)
    for part in range(2):
        for d in (1, 3, 2):
            y_arrival(1, d, part).wait_recv()
    multiply(1, 0)
    combine(0, 2)
    multiply(1, 1)
    multiply(1, 2)
    multiply(0, 4)
    multiply(1, 3)
    multiply(1, 4)
    load_weight.wait()
    load_bias.wait()
    combine(1, 0)
    combine(1, 1)
    combine(1, 2)
    combine(0, 3)
    finish(0)
    combine(1, 3)
    finish(1)

    over(8, lambda o: id_copy(o).wait_send())
    for h in range(2):
        hi_copy(h).wait_send()
        for part in range(2):
            for d in (1, 3, 2):
                y_copy(h, d, part).wait_send()
        for u in range(N_Z + 1):
            over(8, lambda o: x_copy(h, u, o).wait_send())
        for j in range(N_Z - 1):
            z_copy(h, j).wait_send()


def far(count, cols, features, rows, weight, bias, tiles):
    vmem = pl.BlockSpec(memory_space=pltpu.VMEM)
    smem = pl.BlockSpec(memory_space=pltpu.SMEM)
    hbm = pl.BlockSpec(memory_space=pl.ANY)
    dma = pltpu.SemaphoreType.DMA
    return pl.pallas_call(
        far_kernel,
        out_shape=jax.ShapeDtypeStruct((ROWS, 2 * HALF), jnp.bfloat16),
        in_specs=[smem, smem, hbm, hbm, hbm, hbm, hbm],
        out_specs=vmem,
        scratch_shapes=[
            pltpu.VMEM((8 * PER_DEV + 1, BLOCK, HALF), jnp.bfloat16),
            pltpu.VMEM((8 * PER_DEV + 1, BLOCK, HALF), jnp.bfloat16),
            pltpu.VMEM((PER_DEV + 1, BLOCK, 2 * HALF), jnp.bfloat16),
            pltpu.VMEM((PAIRS, BLOCK, BLOCK), jnp.bfloat16),
            pltpu.VMEM((PAIRS, BLOCK, BLOCK), jnp.bfloat16),
            pltpu.VMEM((2 * HALF, 2 * HALF), jnp.bfloat16),
            pltpu.VMEM((1, 2 * HALF), jnp.float32),
            pltpu.VMEM((8, 8, 2 * PAIRS), jnp.float32),
            pltpu.VMEM((N_Z, PER_DEV * GROUP, 8 * LEVELS * GROUP), jnp.bfloat16),
            pltpu.VMEM((PER_DEV * GROUP, PART * GROUP), jnp.bfloat16),
            pltpu.VMEM((PART, BLOCK, 2 * HALF), jnp.bfloat16),
            pltpu.VMEM((PER_DEV, BLOCK, 2 * HALF), jnp.float32),
            pltpu.VMEM((2, N_Z, 7, LEVELS, BLOCK, HALF), jnp.bfloat16),
            pltpu.VMEM((2, N_Z, 8, LEVELS, BLOCK, HALF), jnp.bfloat16),
            pltpu.VMEM((2, N_Z - 1, PER_DEV, BLOCK, HALF), jnp.bfloat16),
            pltpu.VMEM((2, N_Z - 1, PER_DEV, BLOCK, HALF), jnp.bfloat16),
            pltpu.VMEM((2, PER_DEV, BLOCK, HALF), jnp.float32),
            pltpu.VMEM((ROWS, 2 * HALF), jnp.float32),
            dma((6,)),
            dma((2,)),
            dma((2,)),
            dma((2,)),
            dma((2, 2, N_Y - 1)),
            dma((2, 2, N_Y - 1)),
            dma((8,)),
            dma((8,)),
            dma((2, N_Z + 1, 8)),
            dma((2, N_Z + 1, 8)),
            dma((2, N_Z - 1)),
            dma((2, N_Z - 1)),
        ],
        compiler_params=pltpu.CompilerParams(
            collective_id=0, has_side_effects=True, vmem_limit_bytes=60 * 2**20
        ),
    )(count, cols, features, rows, weight, bias, tiles)


def local(features, tile_values, tile_rows, tile_cols, tile_count, weight, bias):
    tiles = tile_values.reshape(PAIRS, 2, BLOCK, BLOCK)
    rows = jnp.broadcast_to(lax.rem(tile_rows, PER_DEV).astype(jnp.float32), (8, 2 * PAIRS))
    blocks = features.reshape(PER_DEV, BLOCK, 2 * HALF)
    return far(tile_count, tile_cols, blocks, rows, weight, bias.reshape(1, -1), tiles)


def solution(mesh):
    return jax.shard_map(
        local,
        mesh=mesh,
        in_specs=(
            P(("row", "col"), None),
            P(("row", "col"), None, None),
            P(("row", "col")),
            P(("row", "col")),
            P(("row", "col")),
            P(),
            P(),
        ),
        out_specs=P(("row", "col"), None),
        check_vma=False,
    )
```

```python
import jax
import jax.numpy as jnp
from jax import lax
from jax.experimental import pallas as pl
from jax.experimental.pallas import tpu as pltpu
from jax.sharding import PartitionSpec as P

MESH = pl.DeviceIdType.MESH
BLOCK = 128
PER_DEV = 16
PAIRS = 128
HALF = 128
ROWS = PER_DEV * BLOCK
GROUP = 16
N_X, N_Z, N_Y, N_HI = 4, 4, 4, 2
LEVELS = 4
SOME = 8
PART = 64
STEPS = (2, 1, 3, 0)


def far_kernel(
    count_ref,
    col_ref,
    feat_ref,
    rows_ref,
    weight_ref,
    bias_ref,
    tiles_ref,
    out_ref,
    gath0,
    gath1,
    feat,
    near_tiles,
    far_tiles,
    weight,
    bias,
    ids,
    pick,
    near_pick,
    near_prod,
    near_sum,
    xs,
    xr,
    zs,
    zr,
    own,
    proj,
    load_sem,
    share_sem,
    hi_send,
    hi_recv,
    y_send,
    y_recv,
    id_send,
    id_recv,
    x_send,
    x_recv,
    z_send,
    z_recv,
):
    row = lax.axis_index("row")
    col = lax.axis_index("col")
    z_hi, y = row // N_Y, lax.rem(row, N_Y)
    x, z, k = col // (2 * N_Z), lax.rem(col // 2, N_Z), lax.rem(col, 2)
    mine = x * 2 + k
    gath = (gath0, gath1)
    live = count_ref[0]

    def plane(o):
        return lax.rem(x + o // 2, N_X) * 2 + lax.rem(k + lax.rem(o, 2), 2)

    def plane_dev(p):
        return {"row": row, "col": (p // 2) * (2 * N_Z) + z * 2 + lax.rem(p, 2)}

    def y_dev(d):
        return {"row": z_hi * N_Y + lax.rem(y + d, N_Y), "col": col}

    hi_row = (1 - z_hi) * N_Y + y
    hi_dev = {"row": hi_row, "col": col}

    def z_dev(d):
        return {"row": row, "col": x * (2 * N_Z) + lax.rem(z + d, N_Z) * 2 + k}

    loads = [
        pltpu.make_async_copy(src, dst, load_sem.at[i])
        for i, (src, dst) in enumerate(
            (
                (feat_ref, feat.at[pl.ds(0, PER_DEV)]),
                (rows_ref, ids.at[mine]),
                (tiles_ref.at[:, 0], near_tiles),
                (tiles_ref.at[:, 1], far_tiles),
                (weight_ref, weight),
                (bias_ref, bias),
            )
        )
    ]
    load_feat, load_rows, load_near, load_far, load_weight, load_bias = loads
    for load in loads:
        load.start()

    barrier = pltpu.get_barrier_semaphore()
    peers = [hi_dev, y_dev(1), y_dev(N_Y - 1)] + [z_dev(d) for d in range(1, N_Z)]
    peers += [plane_dev(plane(o)) for o in range(1, 8)]
    for peer in peers:
        pl.semaphore_signal(barrier, inc=1, device_id=peer, device_id_type=MESH)
    feat[PER_DEV] = jnp.zeros((BLOCK, 2 * HALF), jnp.bfloat16)
    for h in range(2):
        gath[h][8 * PER_DEV] = jnp.zeros((BLOCK, HALF), jnp.bfloat16)
    load_feat.wait()
    load_rows.wait()
    pl.semaphore_wait(barrier, len(peers))

    def share(h, r):
        return gath[h].at[pl.ds(r * PER_DEV, PER_DEV)]

    def half(h):
        return feat.at[pl.ds(0, PER_DEV), :, pl.ds(h * HALF, HALF)]

    def copy(src, dst, send, recv, peer):
        return pltpu.make_async_remote_copy(
            src_ref=src, dst_ref=dst, send_sem=send, recv_sem=recv, device_id=peer, device_id_type=MESH
        )

    def place(h, hi, at_y, first, blocks):
        return gath[h].at[pl.ds((hi * N_Y + at_y) * PER_DEV + first, blocks)]

    def hi_copy(h, c):
        src = feat.at[pl.ds(c * SOME, SOME), :, pl.ds(h * HALF, HALF)]
        return copy(src, place(h, z_hi, y, c * SOME, SOME), hi_send.at[h, c], hi_recv.at[h, c], hi_dev)

    def hi_arrival(h, c):
        dst = place(h, 1 - z_hi, y, c * SOME, SOME)
        return copy(dst, dst, hi_send.at[h, c], hi_recv.at[h, c], hi_dev)

    def piece(t):
        return (z_hi, 0, PER_DEV) if t == 0 else (1 - z_hi, (t - 1) * SOME, SOME)

    def y_copy(h, t, up):
        hi, first, blocks = piece(t)
        dst = place(h, hi, y, first, blocks)
        src = half(h) if t == 0 else dst
        return copy(src, dst, y_send.at[h, t, 0, up], y_recv.at[h, t, 0, up], y_dev(1 if up else N_Y - 1))

    def y_arrival(h, t, up):
        hi, first, blocks = piece(t)
        dst = place(h, hi, lax.rem(y + (N_Y - 1 if up else 1), N_Y), first, blocks)
        return copy(dst, dst, y_send.at[h, t, 0, up], y_recv.at[h, t, 0, up], y_dev(1))

    def on_copy(h, t, up):
        hi, first, blocks = piece(t)
        part = place(h, hi, lax.rem(y + (N_Y - 1 if up else 1), N_Y), first + (1 - up) * (blocks // 2), blocks // 2)
        return copy(part, part, y_send.at[h, t, 1, up], y_recv.at[h, t, 1, up], y_dev(1 if up else N_Y - 1))

    def on_arrival(h, t, up):
        hi, first, blocks = piece(t)
        part = place(h, hi, lax.rem(y + 2, N_Y), first + (1 - up) * (blocks // 2), blocks // 2)
        return copy(part, part, y_send.at[h, t, 1, up], y_recv.at[h, t, 1, up], y_dev(1))

    def send_on(h, t):
        for up in (0, 1):
            y_copy(h, t, up).start()

    def pass_on(h, t):
        for up in (0, 1):
            y_arrival(h, t, up).wait_recv()
            on_copy(h, t, up).start()

    def hi_then_y(h, c):
        hi_arrival(h, c).wait_recv()
        send_on(h, c + 1)

    def gathered(h):
        for t in range(3):
            for up in (0, 1):
                on_arrival(h, t, up).wait_recv()

    def id_copy(o):
        p = plane(o)
        return copy(ids.at[mine], ids.at[mine], id_send.at[p], id_recv.at[mine], plane_dev(p))

    def id_arrival(o):
        p = plane(o)
        return copy(ids.at[p], ids.at[p], id_send.at[p], id_recv.at[p], plane_dev(p))

    def levels(u):
        j = min(u, N_Z - 1)
        return (j, range(LEVELS)) if u < N_Z - 1 else (j, range(2 * (u - j), 2 * (u - j) + 2))

    def x_copy(h, u, o):
        p = plane(o)
        j, lvs = levels(u)
        at = pl.ds(lvs[0], len(lvs))
        return copy(
            xs.at[h, j, o - 1, at], xr.at[h, j, mine, at], x_send.at[h, u, p], x_recv.at[h, u, mine], plane_dev(p)
        )

    def x_arrival(h, u, o):
        p = plane(o)
        j, lvs = levels(u)
        dst = xr.at[h, j, p, pl.ds(lvs[0], len(lvs))]
        return copy(dst, dst, x_send.at[h, u, p], x_recv.at[h, u, p], plane_dev(p))

    def z_copy(h, j):
        return copy(zs.at[h, j], zr.at[h, j], z_send.at[h, j], z_recv.at[h, j], z_dev(STEPS[j]))

    def over(n, body):
        def step(o, carry):
            body(o)
            return carry

        lax.fori_loop(1, n, step, 0)

    hi_copy(0, 0).start()
    hi_copy(0, 1).start()
    send_on(0, 0)
    over(8, lambda o: id_copy(o).start())
    keeps = [pltpu.make_async_copy(half(h), share(h, row), share_sem.at[h]) for h in range(2)]
    for keep in keeps:
        keep.start()

    line = lax.broadcasted_iota(jnp.int32, (PER_DEV * GROUP, BLOCK), 0)
    lane = lax.broadcasted_iota(jnp.int32, (PER_DEV * GROUP, BLOCK), 1)
    same_row = lax.rem(line, GROUP) == lax.rem(lane, GROUP)
    line_block = (line // GROUP).astype(jnp.float32)

    def spread(p, wanted):
        chosen = jnp.where(wanted, 1.0, 0.0).astype(jnp.bfloat16)
        return jnp.dot(ids[p].astype(jnp.bfloat16), chosen, preferred_element_type=jnp.float32)[0:1, :]

    def picker(block):
        return jnp.where(same_row & (line_block == block), 1.0, 0.0).astype(jnp.bfloat16)

    def near(a):
        for c in range(PART * GROUP // BLOCK):
            slot = a * PART + c * (BLOCK // GROUP) + lane // GROUP
            near_pick[:, pl.ds(c * BLOCK, BLOCK)] = picker(spread(mine, line == 2 * slot))

        def multiply_near(s, carry):
            for i in range(4):
                slot = 2 * (a * PART + 4 * s + i)
                src = jnp.where(slot < live, lax.rem(col_ref[slot], PER_DEV), PER_DEV)
                out = jnp.dot(near_tiles[a * PART + 4 * s + i], feat[src], preferred_element_type=jnp.float32)
                near_prod[4 * s + i] = out.astype(jnp.bfloat16)
            return carry

        lax.fori_loop(0, PART // 4, multiply_near, 0)

        def some(g, carry):
            rows = pl.ds(pl.multiple_of(g * GROUP, GROUP), GROUP)
            parts = near_prod[:, rows, :].reshape(PART * GROUP, 2 * HALF)
            total = jnp.dot(near_pick[...], parts, preferred_element_type=jnp.float32)
            total = total.reshape(PER_DEV, GROUP, 2 * HALF)
            near_sum[:, rows, :] = total if a == 0 else near_sum[:, rows, :] + total
            return carry

        lax.fori_loop(0, BLOCK // GROUP, some, 0)

    load_near.wait()
    near(0)
    pass_on(0, 0)
    hi_then_y(0, 0)
    over(8, lambda o: id_arrival(o).wait_recv())
    for j in range(N_Z):
        to = lax.rem(z + STEPS[j], N_Z)
        slot = lax.rem(lane, BLOCK // 2) // GROUP * 32 + x * (2 * N_Z) + to * 2 + k
        for c in range(N_X):
            block = 0.0
            for i in range(2):
                wanted = (line == 2 * slot + 1) & (lane // (BLOCK // 2) == i)
                block += spread(2 * c + i, wanted)
            pick[j, :, pl.ds(c * BLOCK, BLOCK)] = picker(block)

    load_far.wait()
    for keep in keeps:
        keep.wait()
    hi_then_y(0, 1)
    hi_copy(1, 0).start()
    hi_copy(1, 1).start()
    pass_on(0, 1)
    pass_on(0, 2)
    send_on(1, 0)
    gathered(0)

    def product(h, j, p, lv):
        to = lax.rem(z + STEPS[j], N_Z)
        slot = lv * 32 + (p // 2) * (2 * N_Z) + to * 2 + lax.rem(p, 2)
        src = jnp.where(2 * slot + 1 < live, col_ref[2 * slot + 1], 8 * PER_DEV)
        out = jnp.dot(far_tiles[slot], gath[h][src], preferred_element_type=jnp.float32)
        return out.astype(jnp.bfloat16)

    def multiply(h, u):
        j, lvs = levels(u)

        def one(o):
            for lv in lvs:
                xs[h, j, o - 1, lv] = product(h, j, plane(o), lv)
            x_copy(h, u, o).start()

        over(8, one)
        for lv in lvs:
            xr[h, j, mine, lv] = product(h, j, mine, lv)

    def combine(h, j):
        for u in (j,) if j < N_Z - 1 else (j, j + 1):
            over(8, lambda o: x_arrival(h, u, o).wait_recv())

        def some(g, carry):
            rows = pl.ds(pl.multiple_of(g * GROUP, GROUP), GROUP)
            arrived = xr[h, j, :, :, rows, :].reshape(8 * LEVELS * GROUP, HALF)
            total = jnp.dot(pick[j], arrived, preferred_element_type=jnp.float32)
            total = total.reshape(PER_DEV, GROUP, HALF)
            if j < N_Z - 1:
                zs[h, j, :, rows, :] = total.astype(jnp.bfloat16)
            else:
                own[h, :, rows, :] = total
            return carry

        lax.fori_loop(0, BLOCK // GROUP, some, 0)
        if j < N_Z - 1:
            z_copy(h, j).start()

    def finish(h):
        for j in range(N_Z - 1):
            z_copy(h, j).wait_recv()

        def some(b, carry):
            total = own[h, b] + near_sum[b, :, pl.ds(h * HALF, HALF)]
            for j in range(N_Z - 1):
                total += zr[h, j, b].astype(jnp.float32)
            part = jnp.dot(
                total.astype(jnp.bfloat16),
                weight[pl.ds(h * HALF, HALF), :],
                preferred_element_type=jnp.float32,
            )
            rows = pl.ds(pl.multiple_of(b * BLOCK, BLOCK), BLOCK)
            if h == 0:
                proj[rows, :] = part
            else:
                out_ref[rows, :] = jnp.maximum(proj[rows, :] + part + bias[...], 0.0).astype(jnp.bfloat16)
            return carry

        lax.fori_loop(0, PER_DEV, some, 0)

    multiply(0, 0)
    multiply(0, 1)
    hi_then_y(1, 0)
    multiply(0, 2)
    pass_on(1, 0)
    hi_then_y(1, 1)
    multiply(0, 3)
    combine(0, 0)
    pass_on(1, 1)
    pass_on(1, 2)
    combine(0, 1)
    gathered(1)
    multiply(1, 0)
    combine(0, 2)
    multiply(1, 1)
    multiply(1, 2)
    multiply(0, 4)
    multiply(1, 3)
    multiply(1, 4)
    combine(1, 0)
    near(1)
    combine(1, 1)
    load_weight.wait()
    load_bias.wait()
    combine(1, 2)
    combine(0, 3)
    finish(0)
    combine(1, 3)
    finish(1)

    over(8, lambda o: id_copy(o).wait_send())
    for h in range(2):
        for c in range(2):
            hi_copy(h, c).wait_send()
        for t in range(3):
            for up in (0, 1):
                y_copy(h, t, up).wait_send()
                on_copy(h, t, up).wait_send()
        for u in range(N_Z + 1):
            over(8, lambda o: x_copy(h, u, o).wait_send())
        for j in range(N_Z - 1):
            z_copy(h, j).wait_send()


def far(count, cols, features, rows, weight, bias, tiles):
    vmem = pl.BlockSpec(memory_space=pltpu.VMEM)
    smem = pl.BlockSpec(memory_space=pltpu.SMEM)
    hbm = pl.BlockSpec(memory_space=pl.ANY)
    dma = pltpu.SemaphoreType.DMA
    return pl.pallas_call(
        far_kernel,
        out_shape=jax.ShapeDtypeStruct((ROWS, 2 * HALF), jnp.bfloat16),
        in_specs=[smem, smem, hbm, hbm, hbm, hbm, hbm],
        out_specs=vmem,
        scratch_shapes=[
            pltpu.VMEM((8 * PER_DEV + 1, BLOCK, HALF), jnp.bfloat16),
            pltpu.VMEM((8 * PER_DEV + 1, BLOCK, HALF), jnp.bfloat16),
            pltpu.VMEM((PER_DEV + 1, BLOCK, 2 * HALF), jnp.bfloat16),
            pltpu.VMEM((PAIRS, BLOCK, BLOCK), jnp.bfloat16),
            pltpu.VMEM((PAIRS, BLOCK, BLOCK), jnp.bfloat16),
            pltpu.VMEM((2 * HALF, 2 * HALF), jnp.bfloat16),
            pltpu.VMEM((1, 2 * HALF), jnp.float32),
            pltpu.VMEM((8, 8, 2 * PAIRS), jnp.float32),
            pltpu.VMEM((N_Z, PER_DEV * GROUP, 8 * LEVELS * GROUP), jnp.bfloat16),
            pltpu.VMEM((PER_DEV * GROUP, PART * GROUP), jnp.bfloat16),
            pltpu.VMEM((PART, BLOCK, 2 * HALF), jnp.bfloat16),
            pltpu.VMEM((PER_DEV, BLOCK, 2 * HALF), jnp.float32),
            pltpu.VMEM((2, N_Z, 7, LEVELS, BLOCK, HALF), jnp.bfloat16),
            pltpu.VMEM((2, N_Z, 8, LEVELS, BLOCK, HALF), jnp.bfloat16),
            pltpu.VMEM((2, N_Z - 1, PER_DEV, BLOCK, HALF), jnp.bfloat16),
            pltpu.VMEM((2, N_Z - 1, PER_DEV, BLOCK, HALF), jnp.bfloat16),
            pltpu.VMEM((2, PER_DEV, BLOCK, HALF), jnp.float32),
            pltpu.VMEM((ROWS, 2 * HALF), jnp.float32),
            dma((6,)),
            dma((2,)),
            dma((2, 2)),
            dma((2, 2)),
            dma((2, 3, 2, 2)),
            dma((2, 3, 2, 2)),
            dma((8,)),
            dma((8,)),
            dma((2, N_Z + 1, 8)),
            dma((2, N_Z + 1, 8)),
            dma((2, N_Z - 1)),
            dma((2, N_Z - 1)),
        ],
        compiler_params=pltpu.CompilerParams(
            collective_id=0, has_side_effects=True, vmem_limit_bytes=60 * 2**20
        ),
    )(count, cols, features, rows, weight, bias, tiles)


def local(features, tile_values, tile_rows, tile_cols, tile_count, weight, bias):
    tiles = tile_values.reshape(PAIRS, 2, BLOCK, BLOCK)
    rows = jnp.broadcast_to(lax.rem(tile_rows, PER_DEV).astype(jnp.float32), (8, 2 * PAIRS))
    blocks = features.reshape(PER_DEV, BLOCK, 2 * HALF)
    return far(tile_count, tile_cols, blocks, rows, weight, bias.reshape(1, -1), tiles)


def solution(mesh):
    return jax.shard_map(
        local,
        mesh=mesh,
        in_specs=(
            P(("row", "col"), None),
            P(("row", "col"), None, None),
            P(("row", "col")),
            P(("row", "col")),
            P(("row", "col")),
            P(),
            P(),
        ),
        out_specs=P(("row", "col"), None),
        check_vma=False,
    )
```

```python
import jax
import jax.numpy as jnp
from jax import lax
from jax.experimental import pallas as pl
from jax.experimental.pallas import tpu as pltpu
from jax.sharding import PartitionSpec as P

MESH = pl.DeviceIdType.MESH
BLOCK = 128
PER_DEV = 16
PAIRS = 128
HALF = 128
ROWS = PER_DEV * BLOCK
GROUP = 16
N_X, N_Z, N_Y, N_HI = 4, 4, 4, 2
LEVELS = 4
DUOS = 8
SOME = 4
PARTS = 4
PART = 64


def far_kernel(
    count_ref,
    col_ref,
    feat_ref,
    rows_ref,
    weight_ref,
    bias_ref,
    tiles_ref,
    out_ref,
    gath0,
    gath1,
    gath2,
    gath3,
    feat,
    packs,
    near_tiles,
    far_tiles,
    weight,
    bias,
    ids,
    pick,
    near_pick,
    near_prod,
    near_sum,
    xs,
    xr,
    zs,
    zr,
    own,
    proj,
    load_sem,
    share_sem,
    hi_send,
    hi_recv,
    y_send,
    y_recv,
    id_send,
    id_recv,
    x_send,
    x_recv,
    z_send,
    z_recv,
):
    row = lax.axis_index("row")
    col = lax.axis_index("col")
    z_hi, y = row // N_Y, lax.rem(row, N_Y)
    x, z, k = col // (2 * N_Z), lax.rem(col // 2, N_Z), lax.rem(col, 2)
    mine = x * 2 + k
    gath = (gath0, gath1, gath2, gath3)
    live = count_ref[0]
    side = z // 2
    outer = lax.rem(z + 1, N_Z) < 2
    partner = z + 1 - 2 * lax.rem(z, 2)
    far_outer = 3 * (1 - side)
    goals = (2 - side, far_outer, partner, z)

    def plane(o):
        return lax.rem(x + o // 2, N_X) * 2 + lax.rem(k + lax.rem(o, 2), 2)

    def plane_dev(p):
        return {"row": row, "col": (p // 2) * (2 * N_Z) + z * 2 + lax.rem(p, 2)}

    def y_dev(d):
        return {"row": z_hi * N_Y + lax.rem(y + d, N_Y), "col": col}

    hi_row = (1 - z_hi) * N_Y + y
    hi_dev = {"row": hi_row, "col": col}

    def z_dev(to):
        return {"row": row, "col": x * (2 * N_Z) + to * 2 + k}

    loads = [
        pltpu.make_async_copy(src, dst, load_sem.at[i])
        for i, (src, dst) in enumerate(
            (
                (feat_ref, feat.at[pl.ds(0, PER_DEV)]),
                (rows_ref, ids.at[mine]),
                (tiles_ref.at[:, 0], near_tiles),
                (tiles_ref.at[:, 1], far_tiles),
                (weight_ref, weight),
                (bias_ref, bias),
            )
        )
    ]
    load_feat, load_rows, load_near, load_far, load_weight, load_bias = loads
    for load in loads:
        load.start()

    barrier = pltpu.get_barrier_semaphore()
    peers = [hi_dev, y_dev(1), y_dev(N_Y - 1)] + [z_dev(lax.rem(z + d, N_Z)) for d in range(1, N_Z)]
    peers += [plane_dev(plane(o)) for o in range(1, 8)]
    for peer in peers:
        pl.semaphore_signal(barrier, inc=1, device_id=peer, device_id_type=MESH)
    feat[PER_DEV] = jnp.zeros((BLOCK, 2 * HALF), jnp.bfloat16)
    for g in range(PARTS):
        gath[g][8 * DUOS] = jnp.zeros((BLOCK, HALF), jnp.bfloat16)
    low = lax.broadcasted_iota(jnp.int32, (BLOCK, HALF), 1) < HALF // 2

    def swap(value):
        return jnp.concatenate([value[:, HALF // 2 :], value[:, : HALF // 2]], axis=1)

    load_feat.wait()
    for d in range(DUOS):
        for h in range(2):
            even = feat[2 * d, :, pl.ds(h * HALF, HALF)]
            odd = feat[2 * d + 1, :, pl.ds(h * HALF, HALF)]
            packs[2 * h, d] = jnp.where(low, even, swap(odd))
            packs[2 * h + 1, d] = jnp.where(low, swap(even), odd)
    load_rows.wait()
    pl.semaphore_wait(barrier, len(peers))

    def share(g, r):
        return gath[g].at[pl.ds(r * DUOS, DUOS)]

    def copy(src, dst, send, recv, peer):
        return pltpu.make_async_remote_copy(
            src_ref=src, dst_ref=dst, send_sem=send, recv_sem=recv, device_id=peer, device_id_type=MESH
        )

    def place(h, hi, at_y, first, blocks):
        return gath[h].at[pl.ds((hi * N_Y + at_y) * DUOS + first, blocks)]

    def hi_copy(h, c):
        src = packs.at[h, pl.ds(c * SOME, SOME)]
        return copy(src, place(h, z_hi, y, c * SOME, SOME), hi_send.at[h, c], hi_recv.at[h, c], hi_dev)

    def hi_arrival(h, c):
        dst = place(h, 1 - z_hi, y, c * SOME, SOME)
        return copy(dst, dst, hi_send.at[h, c], hi_recv.at[h, c], hi_dev)

    def piece(t):
        return (z_hi, 0, DUOS) if t == 0 else (1 - z_hi, (t - 1) * SOME, SOME)

    def y_copy(h, t, up):
        hi, first, blocks = piece(t)
        dst = place(h, hi, y, first, blocks)
        src = packs.at[h] if t == 0 else dst
        return copy(src, dst, y_send.at[h, t, 0, up], y_recv.at[h, t, 0, up], y_dev(1 if up else N_Y - 1))

    def y_arrival(h, t, up):
        hi, first, blocks = piece(t)
        dst = place(h, hi, lax.rem(y + (N_Y - 1 if up else 1), N_Y), first, blocks)
        return copy(dst, dst, y_send.at[h, t, 0, up], y_recv.at[h, t, 0, up], y_dev(1))

    def on_copy(h, t, up):
        hi, first, blocks = piece(t)
        part = place(h, hi, lax.rem(y + (N_Y - 1 if up else 1), N_Y), first + (1 - up) * (blocks // 2), blocks // 2)
        return copy(part, part, y_send.at[h, t, 1, up], y_recv.at[h, t, 1, up], y_dev(1 if up else N_Y - 1))

    def on_arrival(h, t, up):
        hi, first, blocks = piece(t)
        part = place(h, hi, lax.rem(y + 2, N_Y), first + (1 - up) * (blocks // 2), blocks // 2)
        return copy(part, part, y_send.at[h, t, 1, up], y_recv.at[h, t, 1, up], y_dev(1))

    def send_on(h, t):
        for up in (0, 1):
            y_copy(h, t, up).start()

    def pass_on(h, t):
        for up in (0, 1):
            y_arrival(h, t, up).wait_recv()
            on_copy(h, t, up).start()

    def hi_then_y(h, c):
        hi_arrival(h, c).wait_recv()
        send_on(h, c + 1)

    def gathered(h):
        for t in range(3):
            for up in (0, 1):
                on_arrival(h, t, up).wait_recv()

    def id_copy(o):
        p = plane(o)
        return copy(ids.at[mine], ids.at[mine], id_send.at[p], id_recv.at[mine], plane_dev(p))

    def id_arrival(o):
        p = plane(o)
        return copy(ids.at[p], ids.at[p], id_send.at[p], id_recv.at[p], plane_dev(p))

    def x_copy(g, j, o):
        p = plane(o)
        return copy(xs.at[g, j, o - 1], xr.at[g, j, mine], x_send.at[g, j, p], x_recv.at[g, j, mine], plane_dev(p))

    def x_arrival(g, j, o):
        p = plane(o)
        return copy(xr.at[g, j, p], xr.at[g, j, p], x_send.at[g, j, p], x_recv.at[g, j, p], plane_dev(p))

    def z_copy(h, j):
        peer = jnp.where(outer, partner, far_outer) if j == 1 else goals[j]
        slot = (jnp.where(outer, 1, 2), 0, 3)[j]
        return copy(zs.at[h, j], zr.at[h, slot], z_send.at[h, j], z_recv.at[h, slot], z_dev(peer))

    def z_arrival(h, slot):
        return copy(zr.at[h, slot], zr.at[h, slot], z_send.at[h, 0], z_recv.at[h, slot], z_dev(partner))

    def over(n, body):
        def step(o, carry):
            body(o)
            return carry

        lax.fori_loop(1, n, step, 0)

    hi_copy(0, 0).start()
    hi_copy(0, 1).start()
    send_on(0, 0)
    over(8, lambda o: id_copy(o).start())
    keeps = [pltpu.make_async_copy(packs.at[g], share(g, row), share_sem.at[g]) for g in range(PARTS)]
    for keep in keeps:
        keep.start()

    line = lax.broadcasted_iota(jnp.int32, (PER_DEV * GROUP, BLOCK), 0)
    lane = lax.broadcasted_iota(jnp.int32, (PER_DEV * GROUP, BLOCK), 1)
    same_row = lax.rem(line, GROUP) == lax.rem(lane, GROUP)
    line_block = (line // GROUP).astype(jnp.float32)

    def spread(p, wanted):
        chosen = jnp.where(wanted, 1.0, 0.0).astype(jnp.bfloat16)
        return jnp.dot(ids[p].astype(jnp.bfloat16), chosen, preferred_element_type=jnp.float32)[0:1, :]

    def picker(block):
        return jnp.where(same_row & (line_block == block), 1.0, 0.0).astype(jnp.bfloat16)

    def near(a):
        for c in range(PART * GROUP // BLOCK):
            slot = a * PART + c * (BLOCK // GROUP) + lane // GROUP
            near_pick[:, pl.ds(c * BLOCK, BLOCK)] = picker(spread(mine, line == 2 * slot))

        def multiply_near(s, carry):
            for i in range(4):
                slot = 2 * (a * PART + 4 * s + i)
                src = jnp.where(slot < live, lax.rem(col_ref[slot], PER_DEV), PER_DEV)
                out = jnp.dot(near_tiles[a * PART + 4 * s + i], feat[src], preferred_element_type=jnp.float32)
                near_prod[4 * s + i] = out.astype(jnp.bfloat16)
            return carry

        lax.fori_loop(0, PART // 4, multiply_near, 0)

        def some(g, carry):
            rows = pl.ds(pl.multiple_of(g * GROUP, GROUP), GROUP)
            parts = near_prod[:, rows, :].reshape(PART * GROUP, 2 * HALF)
            total = jnp.dot(near_pick[...], parts, preferred_element_type=jnp.float32)
            total = total.reshape(PER_DEV, GROUP, 2 * HALF)
            near_sum[:, rows, :] = total if a == 0 else near_sum[:, rows, :] + total
            return carry

        lax.fori_loop(0, BLOCK // GROUP, some, 0)

    def build(j):
        to = goals[j]
        level = 2 * (lax.rem(lane, 2 * GROUP) // GROUP)
        for c in range(4):
            slot = (level + c // 2) * 32 + x * (2 * N_Z) + to * 2 + k
            block = 0.0
            for i in range(4):
                wanted = (line == 2 * slot + 1) & (lane // (2 * GROUP) == i)
                block += spread(4 * (c % 2) + i, wanted)
            pick[j, :, pl.ds(c * BLOCK, BLOCK)] = picker(block)

    def product(g, j, p, e):
        to = goals[j]
        left, right = [], []
        for i in range(2):
            slot = (2 * e + i) * 32 + (p // 2) * (2 * N_Z) + to * 2 + lax.rem(p, 2)
            src = jnp.where(2 * slot + 1 < live, col_ref[2 * slot + 1], 8 * PER_DEV)
            block = gath[g][lax.div(src, 2)]
            block = jnp.where(lax.rem(src, 2) == i, block, swap(block))
            left.append(far_tiles[slot])
            right.append(jnp.where(low if i == 0 else ~low, block, jnp.zeros_like(block)))
        out = jnp.dot(
            jnp.concatenate(left, axis=1), jnp.concatenate(right, axis=0), preferred_element_type=jnp.float32
        )
        return out.astype(jnp.bfloat16)

    def multiply(g, j):
        def one(o):
            for e in range(LEVELS // 2):
                xs[g, j, o - 1, e] = product(g, j, plane(o), e)
            x_copy(g, j, o).start()

        over(8, one)
        for e in range(LEVELS // 2):
            xr[g, j, mine, e] = product(g, j, mine, e)

    def combine(h, j):
        for g in (2 * h, 2 * h + 1):
            over(8, lambda o: x_arrival(g, j, o).wait_recv())
        lows = lax.broadcasted_iota(jnp.int32, (8 * LEVELS // 2 * GROUP, HALF), 1) < HALF // 2

        def some(g, carry):
            rows = pl.ds(pl.multiple_of(g * GROUP, GROUP), GROUP)
            one, two = [xr[2 * h + i, j, :, :, rows, :].reshape(8 * LEVELS // 2 * GROUP, HALF) for i in range(2)]
            arrived = [jnp.where(lows, one, swap(two)), jnp.where(lows, swap(one), two)]
            total = jnp.dot(pick[j], jnp.concatenate(arrived, axis=0), preferred_element_type=jnp.float32)
            total = total.reshape(PER_DEV, GROUP, HALF)
            if j < N_Z - 1:
                zs[h, j, :, rows, :] = total.astype(jnp.bfloat16)
            if j % 2:
                own[h, :, rows, :] = total
            return carry

        lax.fori_loop(0, BLOCK // GROUP, some, 0)
        if j == 1:
            pl.when(outer)(z_copy(h, j).start)
        elif j < N_Z - 1:
            z_copy(h, j).start()

    def merge(h):
        @pl.when(jnp.logical_not(outer))
        def _():
            z_arrival(h, 0).wait_recv()

            def some(b, carry):
                zs[h, 1, b] = (own[h, b] + zr[h, 0, b].astype(jnp.float32)).astype(jnp.bfloat16)
                return carry

            lax.fori_loop(0, PER_DEV, some, 0)
            z_copy(h, 1).start()

    def finish(h):
        z_arrival(h, 3).wait_recv()

        @pl.when(outer)
        def _():
            z_arrival(h, 0).wait_recv()

        @pl.when(jnp.logical_not(outer))
        def _():
            z_arrival(h, 1).wait_recv()
            z_arrival(h, 2).wait_recv()

        slots = (3, jnp.where(outer, 0, 1), jnp.where(outer, 4, 2))

        def some(b, carry):
            total = own[h, b] + near_sum[b, :, pl.ds(h * HALF, HALF)]
            for slot in slots:
                total += zr[h, slot, b].astype(jnp.float32)
            part = jnp.dot(
                total.astype(jnp.bfloat16),
                weight[pl.ds(h * HALF, HALF), :],
                preferred_element_type=jnp.float32,
            )
            rows = pl.ds(pl.multiple_of(b * BLOCK, BLOCK), BLOCK)
            if h == 0:
                proj[rows, :] = part
            else:
                out_ref[rows, :] = jnp.maximum(proj[rows, :] + part + bias[...], 0.0).astype(jnp.bfloat16)
            return carry

        lax.fori_loop(0, PER_DEV, some, 0)

    def onward(g):
        pass_on(g, 0)
        hi_then_y(g, 0)
        hi_then_y(g, 1)
        start_hi(g + 1)
        pass_on(g, 1)
        pass_on(g, 2)
        if g + 1 < PARTS:
            send_on(g + 1, 0)

    def start_hi(g):
        if 0 < g < PARTS:
            for c in range(2):
                hi_copy(g, c).start()

    onward(0)
    over(8, lambda o: id_arrival(o).wait_recv())
    build(0)
    load_far.wait()
    for keep in keeps:
        keep.wait()
    gathered(0)
    multiply(0, 0)
    multiply(0, 1)
    pass_on(1, 0)
    hi_then_y(1, 0)
    multiply(0, 2)
    hi_then_y(1, 1)
    start_hi(2)
    build(1)
    pass_on(1, 1)
    pass_on(1, 2)
    send_on(2, 0)
    build(2)
    gathered(1)
    multiply(1, 0)
    multiply(1, 1)
    pass_on(2, 0)
    hi_then_y(2, 0)
    multiply(1, 2)
    hi_then_y(2, 1)
    start_hi(3)
    combine(0, 0)
    pass_on(2, 1)
    pass_on(2, 2)
    send_on(3, 0)
    multiply(0, 3)
    combine(0, 1)
    build(3)
    combine(0, 2)
    gathered(2)
    multiply(2, 0)
    pass_on(3, 0)
    hi_then_y(3, 0)
    multiply(2, 1)
    hi_then_y(3, 1)
    multiply(2, 2)
    merge(0)
    pass_on(3, 1)
    pass_on(3, 2)
    for h in range(2):
        zr[h, 4] = jnp.zeros((PER_DEV, BLOCK, HALF), jnp.bfloat16)
    gathered(3)
    multiply(3, 0)
    multiply(3, 1)
    multiply(3, 2)
    combine(1, 0)
    multiply(1, 3)
    combine(1, 1)
    multiply(2, 3)
    multiply(3, 3)
    combine(1, 2)
    load_near.wait()
    near(0)
    load_weight.wait()
    load_bias.wait()
    merge(1)
    near(1)
    combine(0, 3)
    finish(0)
    combine(1, 3)
    finish(1)

    over(8, lambda o: id_copy(o).wait_send())
    for g in range(PARTS):
        for c in range(2):
            hi_copy(g, c).wait_send()
        for t in range(3):
            for up in (0, 1):
                y_copy(g, t, up).wait_send()
                on_copy(g, t, up).wait_send()
        for j in range(N_Z):
            over(8, lambda o: x_copy(g, j, o).wait_send())
    for h in range(2):
        for j in range(N_Z - 1):
            z_copy(h, j).wait_send()


def far(count, cols, features, rows, weight, bias, tiles):
    vmem = pl.BlockSpec(memory_space=pltpu.VMEM)
    smem = pl.BlockSpec(memory_space=pltpu.SMEM)
    hbm = pl.BlockSpec(memory_space=pl.ANY)
    dma = pltpu.SemaphoreType.DMA
    return pl.pallas_call(
        far_kernel,
        out_shape=jax.ShapeDtypeStruct((ROWS, 2 * HALF), jnp.bfloat16),
        in_specs=[smem, smem, hbm, hbm, hbm, hbm, hbm],
        out_specs=vmem,
        scratch_shapes=[
            *[pltpu.VMEM((8 * DUOS + 1, BLOCK, HALF), jnp.bfloat16)] * PARTS,
            pltpu.VMEM((PER_DEV + 1, BLOCK, 2 * HALF), jnp.bfloat16),
            pltpu.VMEM((PARTS, DUOS, BLOCK, HALF), jnp.bfloat16),
            pltpu.VMEM((PAIRS, BLOCK, BLOCK), jnp.bfloat16),
            pltpu.VMEM((PAIRS, BLOCK, BLOCK), jnp.bfloat16),
            pltpu.VMEM((2 * HALF, 2 * HALF), jnp.bfloat16),
            pltpu.VMEM((1, 2 * HALF), jnp.float32),
            pltpu.VMEM((8, 8, 2 * PAIRS), jnp.float32),
            pltpu.VMEM((N_Z, PER_DEV * GROUP, 8 * LEVELS * GROUP), jnp.bfloat16),
            pltpu.VMEM((PER_DEV * GROUP, PART * GROUP), jnp.bfloat16),
            pltpu.VMEM((PART, BLOCK, 2 * HALF), jnp.bfloat16),
            pltpu.VMEM((PER_DEV, BLOCK, 2 * HALF), jnp.float32),
            pltpu.VMEM((PARTS, N_Z, 7, LEVELS // 2, BLOCK, HALF), jnp.bfloat16),
            pltpu.VMEM((PARTS, N_Z, 8, LEVELS // 2, BLOCK, HALF), jnp.bfloat16),
            pltpu.VMEM((2, N_Z - 1, PER_DEV, BLOCK, HALF), jnp.bfloat16),
            pltpu.VMEM((2, N_Z + 1, PER_DEV, BLOCK, HALF), jnp.bfloat16),
            pltpu.VMEM((2, PER_DEV, BLOCK, HALF), jnp.float32),
            pltpu.VMEM((ROWS, 2 * HALF), jnp.float32),
            dma((6,)),
            dma((PARTS,)),
            dma((PARTS, 2)),
            dma((PARTS, 2)),
            dma((PARTS, 3, 2, 2)),
            dma((PARTS, 3, 2, 2)),
            dma((8,)),
            dma((8,)),
            dma((PARTS, N_Z, 8)),
            dma((PARTS, N_Z, 8)),
            dma((2, N_Z - 1)),
            dma((2, N_Z)),
        ],
        compiler_params=pltpu.CompilerParams(
            collective_id=0, has_side_effects=True, vmem_limit_bytes=60 * 2**20
        ),
    )(count, cols, features, rows, weight, bias, tiles)


def local(features, tile_values, tile_rows, tile_cols, tile_count, weight, bias):
    tiles = tile_values.reshape(PAIRS, 2, BLOCK, BLOCK)
    rows = jnp.broadcast_to(lax.rem(tile_rows, PER_DEV).astype(jnp.float32), (8, 2 * PAIRS))
    blocks = features.reshape(PER_DEV, BLOCK, 2 * HALF)
    return far(tile_count, tile_cols, blocks, rows, weight, bias.reshape(1, -1), tiles)


def solution(mesh):
    return jax.shard_map(
        local,
        mesh=mesh,
        in_specs=(
            P(("row", "col"), None),
            P(("row", "col"), None, None),
            P(("row", "col")),
            P(("row", "col")),
            P(("row", "col")),
            P(),
            P(),
        ),
        out_specs=P(("row", "col"), None),
        check_vma=False,
    )
```

```python
import jax
import jax.numpy as jnp
from jax import lax
from jax.experimental import pallas as pl
from jax.experimental.pallas import tpu as pltpu
from jax.sharding import PartitionSpec as P

MESH = pl.DeviceIdType.MESH
BLOCK = 128
PER_DEV = 16
PAIRS = 128
HALF = 128
ROWS = PER_DEV * BLOCK
GROUP = 16
N_X, N_Z, N_Y, N_HI = 4, 4, 4, 2
LEVELS = 4
DUOS = 8
SOME = 4
PARTS = 4
PART = 64


def far_kernel(
    count_ref,
    col_ref,
    feat_ref,
    rows_ref,
    weight_ref,
    bias_ref,
    tiles_ref,
    out_ref,
    gath0,
    gath1,
    gath2,
    gath3,
    feat,
    packs,
    near_tiles,
    far_tiles,
    weight,
    bias,
    ids,
    pick,
    near_pick,
    near_prod,
    near_sum,
    xs,
    xr,
    zs,
    zr,
    own,
    proj,
    load_sem,
    share_sem,
    hi_send,
    hi_recv,
    y_send,
    y_recv,
    id_send,
    id_recv,
    x_send,
    x_recv,
    z_send,
    z_recv,
):
    row = lax.axis_index("row")
    col = lax.axis_index("col")
    z_hi, y = row // N_Y, lax.rem(row, N_Y)
    x, z, k = col // (2 * N_Z), lax.rem(col // 2, N_Z), lax.rem(col, 2)
    mine = x * 2 + k
    gath = (gath0, gath1, gath2, gath3)
    live = count_ref[0]
    side = z // 2
    outer = lax.rem(z + 1, N_Z) < 2
    partner = z + 1 - 2 * lax.rem(z, 2)
    far_outer = 3 * (1 - side)
    goals = (2 - side, far_outer, partner, z)

    def plane(o):
        return lax.rem(x + o // 2, N_X) * 2 + lax.rem(k + lax.rem(o, 2), 2)

    def plane_dev(p):
        return {"row": row, "col": (p // 2) * (2 * N_Z) + z * 2 + lax.rem(p, 2)}

    def y_dev(d):
        return {"row": z_hi * N_Y + lax.rem(y + d, N_Y), "col": col}

    hi_row = (1 - z_hi) * N_Y + y
    hi_dev = {"row": hi_row, "col": col}

    def z_dev(to):
        return {"row": row, "col": x * (2 * N_Z) + to * 2 + k}

    loads = [
        pltpu.make_async_copy(src, dst, load_sem.at[i])
        for i, (src, dst) in enumerate(
            (
                (feat_ref, feat.at[pl.ds(0, PER_DEV)]),
                (rows_ref, ids.at[mine]),
                (tiles_ref.at[:, 0], near_tiles),
                (tiles_ref.at[:, 1], far_tiles),
                (weight_ref, weight),
                (bias_ref, bias),
            )
        )
    ]
    load_feat, load_rows, load_near, load_far, load_weight, load_bias = loads
    for load in loads:
        load.start()

    barrier = pltpu.get_barrier_semaphore()
    peers = [hi_dev, y_dev(1), y_dev(N_Y - 1)] + [z_dev(lax.rem(z + d, N_Z)) for d in range(1, N_Z)]
    peers += [plane_dev(plane(o)) for o in range(1, 8)]
    for peer in peers:
        pl.semaphore_signal(barrier, inc=1, device_id=peer, device_id_type=MESH)
    feat[PER_DEV] = jnp.zeros((BLOCK, 2 * HALF), jnp.bfloat16)
    for g in range(PARTS):
        gath[g][8 * DUOS] = jnp.zeros((BLOCK, HALF), jnp.bfloat16)
    low = lax.broadcasted_iota(jnp.int32, (BLOCK, HALF), 1) < HALF // 2

    def swap(value):
        return jnp.concatenate([value[:, HALF // 2 :], value[:, : HALF // 2]], axis=1)

    load_feat.wait()
    for d in range(DUOS):
        for h in range(2):
            even = feat[2 * d, :, pl.ds(h * HALF, HALF)]
            odd = feat[2 * d + 1, :, pl.ds(h * HALF, HALF)]
            packs[2 * h, d] = jnp.where(low, even, swap(odd))
            packs[2 * h + 1, d] = jnp.where(low, swap(even), odd)
    load_rows.wait()
    pl.semaphore_wait(barrier, len(peers))

    def share(g, r):
        return gath[g].at[pl.ds(r * DUOS, DUOS)]

    def copy(src, dst, send, recv, peer):
        return pltpu.make_async_remote_copy(
            src_ref=src, dst_ref=dst, send_sem=send, recv_sem=recv, device_id=peer, device_id_type=MESH
        )

    def place(h, hi, at_y, first, blocks):
        return gath[h].at[pl.ds((hi * N_Y + at_y) * DUOS + first, blocks)]

    def hi_copy(h, c):
        src = packs.at[h, pl.ds(c * SOME, SOME)]
        return copy(src, place(h, z_hi, y, c * SOME, SOME), hi_send.at[h, c], hi_recv.at[h, c], hi_dev)

    def hi_arrival(h, c):
        dst = place(h, 1 - z_hi, y, c * SOME, SOME)
        return copy(dst, dst, hi_send.at[h, c], hi_recv.at[h, c], hi_dev)

    def piece(t):
        return (z_hi, 0, DUOS) if t == 0 else (1 - z_hi, (t - 1) * SOME, SOME)

    def y_copy(h, t, up):
        hi, first, blocks = piece(t)
        dst = place(h, hi, y, first, blocks)
        src = packs.at[h] if t == 0 else dst
        return copy(src, dst, y_send.at[h, t, 0, up], y_recv.at[h, t, 0, up], y_dev(1 if up else N_Y - 1))

    def y_arrival(h, t, up):
        hi, first, blocks = piece(t)
        dst = place(h, hi, lax.rem(y + (N_Y - 1 if up else 1), N_Y), first, blocks)
        return copy(dst, dst, y_send.at[h, t, 0, up], y_recv.at[h, t, 0, up], y_dev(1))

    def on_copy(h, t, up):
        hi, first, blocks = piece(t)
        part = place(h, hi, lax.rem(y + (N_Y - 1 if up else 1), N_Y), first + (1 - up) * (blocks // 2), blocks // 2)
        return copy(part, part, y_send.at[h, t, 1, up], y_recv.at[h, t, 1, up], y_dev(1 if up else N_Y - 1))

    def on_arrival(h, t, up):
        hi, first, blocks = piece(t)
        part = place(h, hi, lax.rem(y + 2, N_Y), first + (1 - up) * (blocks // 2), blocks // 2)
        return copy(part, part, y_send.at[h, t, 1, up], y_recv.at[h, t, 1, up], y_dev(1))

    def send_on(h, t):
        for up in (0, 1):
            y_copy(h, t, up).start()

    def pass_on(h, t):
        for up in (0, 1):
            y_arrival(h, t, up).wait_recv()
            on_copy(h, t, up).start()

    def hi_then_y(h, c):
        hi_arrival(h, c).wait_recv()
        send_on(h, c + 1)

    def gathered(h):
        for t in range(3):
            for up in (0, 1):
                on_arrival(h, t, up).wait_recv()

    def id_copy(o):
        p = plane(o)
        return copy(ids.at[mine], ids.at[mine], id_send.at[p], id_recv.at[mine], plane_dev(p))

    def id_arrival(o):
        p = plane(o)
        return copy(ids.at[p], ids.at[p], id_send.at[p], id_recv.at[p], plane_dev(p))

    def x_copy(g, j, o):
        p = plane(o)
        return copy(xs.at[g, j, o - 1], xr.at[g, j, mine], x_send.at[g, j, p], x_recv.at[g, j, mine], plane_dev(p))

    def x_arrival(g, j, o):
        p = plane(o)
        return copy(xr.at[g, j, p], xr.at[g, j, p], x_send.at[g, j, p], x_recv.at[g, j, p], plane_dev(p))

    def z_copy(h, j):
        peer = jnp.where(outer, partner, far_outer) if j == 1 else goals[j]
        slot = (jnp.where(outer, 1, 2), 0, 3)[j]
        return copy(zs.at[h, j], zr.at[h, slot], z_send.at[h, j], z_recv.at[h, slot], z_dev(peer))

    def z_arrival(h, slot):
        return copy(zr.at[h, slot], zr.at[h, slot], z_send.at[h, 0], z_recv.at[h, slot], z_dev(partner))

    def over(n, body):
        def step(o, carry):
            body(o)
            return carry

        lax.fori_loop(1, n, step, 0)

    hi_copy(0, 0).start()
    hi_copy(0, 1).start()
    send_on(0, 0)
    over(8, lambda o: id_copy(o).start())
    keeps = [pltpu.make_async_copy(packs.at[g], share(g, row), share_sem.at[g]) for g in range(PARTS)]
    for keep in keeps:
        keep.start()

    line = lax.broadcasted_iota(jnp.int32, (PER_DEV * GROUP, BLOCK), 0)
    lane = lax.broadcasted_iota(jnp.int32, (PER_DEV * GROUP, BLOCK), 1)
    same_row = lax.rem(line, GROUP) == lax.rem(lane, GROUP)
    line_block = (line // GROUP).astype(jnp.float32)

    def spread(p, wanted):
        chosen = jnp.where(wanted, 1.0, 0.0).astype(jnp.bfloat16)
        return jnp.dot(ids[p].astype(jnp.bfloat16), chosen, preferred_element_type=jnp.float32)[0:1, :]

    def picker(block):
        return jnp.where(same_row & (line_block == block), 1.0, 0.0).astype(jnp.bfloat16)

    def near(a):
        for c in range(PART * GROUP // BLOCK):
            slot = a * PART + c * (BLOCK // GROUP) + lane // GROUP
            near_pick[:, pl.ds(c * BLOCK, BLOCK)] = picker(spread(mine, line == 2 * slot))

        def multiply_near(s, carry):
            for i in range(4):
                slot = 2 * (a * PART + 4 * s + i)
                src = jnp.where(slot < live, lax.rem(col_ref[slot], PER_DEV), PER_DEV)
                out = jnp.dot(near_tiles[a * PART + 4 * s + i], feat[src], preferred_element_type=jnp.float32)
                near_prod[4 * s + i] = out.astype(jnp.bfloat16)
            return carry

        lax.fori_loop(0, PART // 4, multiply_near, 0)

        def some(g, carry):
            rows = pl.ds(pl.multiple_of(g * GROUP, GROUP), GROUP)
            parts = near_prod[:, rows, :].reshape(PART * GROUP, 2 * HALF)
            total = jnp.dot(near_pick[...], parts, preferred_element_type=jnp.float32)
            total = total.reshape(PER_DEV, GROUP, 2 * HALF)
            near_sum[:, rows, :] = total if a == 0 else near_sum[:, rows, :] + total
            return carry

        lax.fori_loop(0, BLOCK // GROUP, some, 0)

    def build(j):
        to = goals[j]
        level = 2 * (lax.rem(lane, 2 * GROUP) // GROUP)
        for c in range(4):
            slot = (level + c // 2) * 32 + x * (2 * N_Z) + to * 2 + k
            block = 0.0
            for i in range(4):
                wanted = (line == 2 * slot + 1) & (lane // (2 * GROUP) == i)
                block += spread(4 * (c % 2) + i, wanted)
            pick[j, :, pl.ds(c * BLOCK, BLOCK)] = picker(block)

    def product(g, j, p, e):
        to = goals[j]
        left, right = [], []
        for i in range(2):
            slot = (2 * e + i) * 32 + (p // 2) * (2 * N_Z) + to * 2 + lax.rem(p, 2)
            src = jnp.where(2 * slot + 1 < live, col_ref[2 * slot + 1], 8 * PER_DEV)
            block = gath[g][lax.div(src, 2)]
            block = jnp.where(lax.rem(src, 2) == i, block, swap(block))
            left.append(far_tiles[slot])
            right.append(jnp.where(low if i == 0 else ~low, block, jnp.zeros_like(block)))
        out = jnp.dot(
            jnp.concatenate(left, axis=1), jnp.concatenate(right, axis=0), preferred_element_type=jnp.float32
        )
        return out.astype(jnp.bfloat16)

    def multiply(g, j):
        def one(o):
            for e in range(LEVELS // 2):
                xs[g, j, o - 1, e] = product(g, j, plane(o), e)
            x_copy(g, j, o).start()

        over(8, one)
        for e in range(LEVELS // 2):
            xr[g, j, mine, e] = product(g, j, mine, e)

    def combine(h, j):
        for g in (2 * h, 2 * h + 1):
            over(8, lambda o: x_arrival(g, j, o).wait_recv())
        lows = lax.broadcasted_iota(jnp.int32, (8 * LEVELS // 2 * GROUP, HALF), 1) < HALF // 2

        def some(g, carry):
            rows = pl.ds(pl.multiple_of(g * GROUP, GROUP), GROUP)
            one, two = [xr[2 * h + i, j, :, :, rows, :].reshape(8 * LEVELS // 2 * GROUP, HALF) for i in range(2)]
            arrived = [jnp.where(lows, one, swap(two)), jnp.where(lows, swap(one), two)]
            total = jnp.dot(pick[j], jnp.concatenate(arrived, axis=0), preferred_element_type=jnp.float32)
            total = total.reshape(PER_DEV, GROUP, HALF)
            if j < N_Z - 1:
                zs[h, j, :, rows, :] = total.astype(jnp.bfloat16)
            if j % 2:
                own[h, :, rows, :] = total
            return carry

        lax.fori_loop(0, BLOCK // GROUP, some, 0)
        if j == 1:
            pl.when(outer)(z_copy(h, j).start)
        elif j < N_Z - 1:
            z_copy(h, j).start()

    def merge(h):
        @pl.when(jnp.logical_not(outer))
        def _():
            z_arrival(h, 0).wait_recv()

            def some(b, carry):
                zs[h, 1, b] = (own[h, b] + zr[h, 0, b].astype(jnp.float32)).astype(jnp.bfloat16)
                return carry

            lax.fori_loop(0, PER_DEV, some, 0)
            z_copy(h, 1).start()

    def finish(h):
        z_arrival(h, 3).wait_recv()

        @pl.when(outer)
        def _():
            z_arrival(h, 0).wait_recv()

        @pl.when(jnp.logical_not(outer))
        def _():
            z_arrival(h, 1).wait_recv()
            z_arrival(h, 2).wait_recv()

        slots = (3, jnp.where(outer, 0, 1), jnp.where(outer, 4, 2))

        def some(b, carry):
            total = own[h, b] + near_sum[b, :, pl.ds(h * HALF, HALF)]
            for slot in slots:
                total += zr[h, slot, b].astype(jnp.float32)
            part = jnp.dot(
                total.astype(jnp.bfloat16),
                weight[pl.ds(h * HALF, HALF), :],
                preferred_element_type=jnp.float32,
            )
            rows = pl.ds(pl.multiple_of(b * BLOCK, BLOCK), BLOCK)
            if h == 0:
                proj[rows, :] = part
            else:
                out_ref[rows, :] = jnp.maximum(proj[rows, :] + part + bias[...], 0.0).astype(jnp.bfloat16)
            return carry

        lax.fori_loop(0, PER_DEV, some, 0)

    def onward(g):
        pass_on(g, 0)
        hi_then_y(g, 0)
        hi_then_y(g, 1)
        start_hi(g + 1)
        pass_on(g, 1)
        pass_on(g, 2)
        if g + 1 < PARTS:
            send_on(g + 1, 0)

    def start_hi(g):
        if 0 < g < PARTS:
            for c in range(2):
                hi_copy(g, c).start()

    onward(0)
    over(8, lambda o: id_arrival(o).wait_recv())
    build(0)
    load_far.wait()
    for keep in keeps:
        keep.wait()
    gathered(0)
    multiply(0, 0)
    multiply(0, 1)
    pass_on(1, 0)
    hi_then_y(1, 0)
    multiply(0, 2)
    hi_then_y(1, 1)
    start_hi(2)
    build(1)
    pass_on(1, 1)
    pass_on(1, 2)
    send_on(2, 0)
    build(2)
    gathered(1)
    multiply(1, 0)
    pass_on(2, 0)
    hi_then_y(2, 0)
    multiply(1, 1)
    hi_then_y(2, 1)
    start_hi(3)
    multiply(1, 2)
    combine(0, 0)
    pass_on(2, 1)
    pass_on(2, 2)
    send_on(3, 0)
    multiply(0, 3)
    combine(0, 1)
    build(3)
    gathered(2)
    multiply(2, 0)
    pass_on(3, 0)
    hi_then_y(3, 0)
    hi_then_y(3, 1)
    multiply(2, 1)
    combine(0, 2)
    multiply(2, 2)
    pass_on(3, 1)
    pass_on(3, 2)
    zr[0, 4] = jnp.zeros((PER_DEV, BLOCK, HALF), jnp.bfloat16)
    zr[1, 4] = jnp.zeros((PER_DEV, BLOCK, HALF), jnp.bfloat16)
    merge(0)
    gathered(3)
    multiply(3, 0)
    multiply(3, 1)
    multiply(3, 2)
    combine(1, 0)
    multiply(1, 3)
    combine(1, 1)
    multiply(2, 3)
    multiply(3, 3)
    combine(1, 2)
    load_near.wait()
    near(0)
    load_weight.wait()
    load_bias.wait()
    merge(1)
    near(1)
    combine(0, 3)
    finish(0)
    combine(1, 3)
    finish(1)

    over(8, lambda o: id_copy(o).wait_send())
    for g in range(PARTS):
        for c in range(2):
            hi_copy(g, c).wait_send()
        for t in range(3):
            for up in (0, 1):
                y_copy(g, t, up).wait_send()
                on_copy(g, t, up).wait_send()
        for j in range(N_Z):
            over(8, lambda o: x_copy(g, j, o).wait_send())
    for h in range(2):
        for j in range(N_Z - 1):
            z_copy(h, j).wait_send()


def far(count, cols, features, rows, weight, bias, tiles):
    vmem = pl.BlockSpec(memory_space=pltpu.VMEM)
    smem = pl.BlockSpec(memory_space=pltpu.SMEM)
    hbm = pl.BlockSpec(memory_space=pl.ANY)
    dma = pltpu.SemaphoreType.DMA
    return pl.pallas_call(
        far_kernel,
        out_shape=jax.ShapeDtypeStruct((ROWS, 2 * HALF), jnp.bfloat16),
        in_specs=[smem, smem, hbm, hbm, hbm, hbm, hbm],
        out_specs=vmem,
        scratch_shapes=[
            *[pltpu.VMEM((8 * DUOS + 1, BLOCK, HALF), jnp.bfloat16)] * PARTS,
            pltpu.VMEM((PER_DEV + 1, BLOCK, 2 * HALF), jnp.bfloat16),
            pltpu.VMEM((PARTS, DUOS, BLOCK, HALF), jnp.bfloat16),
            pltpu.VMEM((PAIRS, BLOCK, BLOCK), jnp.bfloat16),
            pltpu.VMEM((PAIRS, BLOCK, BLOCK), jnp.bfloat16),
            pltpu.VMEM((2 * HALF, 2 * HALF), jnp.bfloat16),
            pltpu.VMEM((1, 2 * HALF), jnp.float32),
            pltpu.VMEM((8, 8, 2 * PAIRS), jnp.float32),
            pltpu.VMEM((N_Z, PER_DEV * GROUP, 8 * LEVELS * GROUP), jnp.bfloat16),
            pltpu.VMEM((PER_DEV * GROUP, PART * GROUP), jnp.bfloat16),
            pltpu.VMEM((PART, BLOCK, 2 * HALF), jnp.bfloat16),
            pltpu.VMEM((PER_DEV, BLOCK, 2 * HALF), jnp.float32),
            pltpu.VMEM((PARTS, N_Z, 7, LEVELS // 2, BLOCK, HALF), jnp.bfloat16),
            pltpu.VMEM((PARTS, N_Z, 8, LEVELS // 2, BLOCK, HALF), jnp.bfloat16),
            pltpu.VMEM((2, N_Z - 1, PER_DEV, BLOCK, HALF), jnp.bfloat16),
            pltpu.VMEM((2, N_Z + 1, PER_DEV, BLOCK, HALF), jnp.bfloat16),
            pltpu.VMEM((2, PER_DEV, BLOCK, HALF), jnp.float32),
            pltpu.VMEM((ROWS, 2 * HALF), jnp.float32),
            dma((6,)),
            dma((PARTS,)),
            dma((PARTS, 2)),
            dma((PARTS, 2)),
            dma((PARTS, 3, 2, 2)),
            dma((PARTS, 3, 2, 2)),
            dma((8,)),
            dma((8,)),
            dma((PARTS, N_Z, 8)),
            dma((PARTS, N_Z, 8)),
            dma((2, N_Z - 1)),
            dma((2, N_Z)),
        ],
        compiler_params=pltpu.CompilerParams(
            collective_id=0, has_side_effects=True, vmem_limit_bytes=60 * 2**20
        ),
    )(count, cols, features, rows, weight, bias, tiles)


def local(features, tile_values, tile_rows, tile_cols, tile_count, weight, bias):
    tiles = tile_values.reshape(PAIRS, 2, BLOCK, BLOCK)
    rows = jnp.broadcast_to(lax.rem(tile_rows, PER_DEV).astype(jnp.float32), (8, 2 * PAIRS))
    blocks = features.reshape(PER_DEV, BLOCK, 2 * HALF)
    return far(tile_count, tile_cols, blocks, rows, weight, bias.reshape(1, -1), tiles)


def solution(mesh):
    return jax.shard_map(
        local,
        mesh=mesh,
        in_specs=(
            P(("row", "col"), None),
            P(("row", "col"), None, None),
            P(("row", "col")),
            P(("row", "col")),
            P(("row", "col")),
            P(),
            P(),
        ),
        out_specs=P(("row", "col"), None),
        check_vma=False,
    )
```
